32 devices in a mesh: wide: 8 (over y, x, core), narrow: 4 (over z).
Axes of the slice: x: 2, y: 2, z: 4, core: 2. Of those that a mesh axis runs over, the one named last changes fastest.
Arguments:
- inputs: bfloat16 [896, 16384], P('wide', 'narrow'), may hold values from -6 to 6
- grad_out: bfloat16 [896, 53248], P('narrow', 'wide'), may hold values from -6 to 6
- w_base: bfloat16 [16384, 53248], P('narrow', 'wide'), may hold values from -0.046875 to 0.046875
- adapter_down_matrix: bfloat16 [16384, 256], P('narrow'), may hold values from -0.046875 to 0.046875
- b_factor: bfloat16 [256, 53248], P(None, 'wide'), may hold values from -0.375 to 0.375
Outputs:
- input_gradient: bfloat16 [896, 16384], P('wide', 'narrow')
- grad_a: float32 [16384, 256], P('narrow')
- grad_b: float32 [256, 53248], P(None, 'wide')
The draws below stay inside these ranges and needn't reach their ends.
All inputs are finite; a program needn't handle non-finite values.
Results may differ from the reference program's by a relative error of at most 0.0046.
Values may be sent and summed in bfloat16 or wider, within the bound.
No kernel may reach another device: no remote copies, remote signals or barrier semaphores. Data moves between devices by JAX's collectives and lax.ppermute only.
A program may use at most 192 MiB of HBM per device.

```python
import jax
import jax.numpy as jnp

D = 16384
F = 53248
R = 256
TOKEN_COUNT = 896


def spiked(values, key, source, target, shards_of, factor):
    def block_of(axis_at):
        return (jnp.arange(values.shape[axis_at]) // (values.shape[axis_at] // shards_of)).reshape((-1,) + (1,) * (values.ndim - 1 - axis_at))

    first = jax.random.permutation(key, shards_of)[block_of(target)]
    other_side = (block_of(target) + shards_of // 2) % shards_of
    return jnp.where((block_of(source) == first) | (block_of(source) == other_side), factor * values, values)


def levels(key, dims, pieces, least, largest):
    factor_of, own = 1.0, jax.random.fold_in(key, 6)
    for dim, shards_of in pieces:
        draws = jnp.exp(jax.random.uniform(jax.random.fold_in(own, dim), (shards_of,), jnp.float32, least / len(pieces), largest / len(pieces)))
        factor_of = factor_of * jnp.repeat(draws, dims[dim] // shards_of).reshape([-1 if axis == dim else 1 for axis in range(len(dims))])
    return factor_of


def noise(key, shape, scale, bound, split=(), kind=jnp.bfloat16):
    values = jax.random.normal(key, shape, jnp.float32) * scale
    if len(split) > 0:
        values = levels(key, shape, split, -0.22, 0.18) * values
    return jnp.clip(values, min=-bound, max=bound).astype(kind)


def bell_draw_with(stream_key, extent, deviation, limit, split, heavy, dtype=jnp.bfloat16):
    entries = deviation * jax.random.normal(stream_key, extent, jnp.float32)
    if split:
        entries = entries * levels(stream_key, extent, split, -0.22, 0.18)
    return jnp.clip(spiked(entries, jax.random.fold_in(stream_key, 3), *heavy), -limit, limit).astype(dtype)


def setup_inputs(seed: int = 0) -> dict:
    key_list = jax.random.split(jax.random.key(seed), 6)
    inputs = noise(key_list[0], (TOKEN_COUNT, D), 1.0, 6.0, ((0, 8), (1, 4)))
    grad_out = bell_draw_with(key_list[1], (TOKEN_COUNT, F), 1.0, 6.0, ((0, 4), (1, 8)), (1, 0, 8, 2.0))
    w_base = noise(key_list[2], (D, F), D ** -0.5, 0.046875, ((0, 4), (1, 8)))
    adapter_down_matrix = noise(key_list[3], (D, R), D ** -0.5, 0.046875, ((0, 4),))
    b_factor = noise(key_list[4], (R, F), R ** -0.5, 0.375, ((1, 8),))
    return dict(inputs=inputs, grad_out=grad_out, w_base=w_base, adapter_down_matrix=adapter_down_matrix, b_factor=b_factor)


adapter_scale = 2.0


def reference(inputs, grad_out, w_base, adapter_down_matrix, b_factor):
    frozen_input_gradient = jnp.dot(grad_out, w_base.T, preferred_element_type=jnp.float32)
    low_rank_gradient = jnp.dot(grad_out, b_factor.T, preferred_element_type=jnp.float32).astype(jnp.bfloat16)
    input_gradient = (frozen_input_gradient + adapter_scale * jnp.dot(low_rank_gradient, adapter_down_matrix.T, preferred_element_type=jnp.float32)).astype(jnp.bfloat16)
    adapter_matrix = adapter_scale / TOKEN_COUNT
    grad_a = adapter_matrix * jnp.dot(inputs.T, low_rank_gradient, preferred_element_type=jnp.float32)
    low_act = jnp.dot(inputs, adapter_down_matrix, preferred_element_type=jnp.float32).astype(jnp.bfloat16)
    grad_b = adapter_matrix * jnp.dot(low_act.T, grad_out, preferred_element_type=jnp.float32)
    return input_gradient, grad_a, grad_b
```

```python
import jax
import jax.numpy as jnp
from jax import lax
from jax.sharding import PartitionSpec as P

adapter_scale = 2.0
piece_rows = 32


def contract_trailing_axis(left, right):
    return lax.dot_general(
        left, right, (((1,), (1,)), ((), ())), preferred_element_type=jnp.float32
    )


def contract_first(left, right):
    return lax.dot_general(
        left, right, (((0,), (0,)), ((), ())), preferred_element_type=jnp.float32
    )


def swap(value, axis, bit):
    size = lax.axis_size(axis)
    return lax.ppermute(value, axis, [(i, i ^ bit) for i in range(size)])


def shift(value, axis, by):
    size = lax.axis_size(axis)
    return lax.ppermute(value, axis, [(i, (i + by) % size) for i in range(size)])


def sum_over(value, axis):
    bit = 1
    while bit < lax.axis_size(axis):
        value = value + swap(value, axis, bit)
        bit *= 2
    return value


def gather_over(value, axis):
    me = lax.axis_index(axis)
    bit = 1
    while bit < lax.axis_size(axis):
        other = swap(value, axis, bit)
        upper = (me & bit) != 0
        first = jnp.where(upper, other, value)
        second = jnp.where(upper, value, other)
        value = jnp.concatenate([first, second], axis=0)
        bit *= 2
    return value


def ring_gather(block, axis):
    size = lax.axis_size(axis)
    found = {0: block}
    up = down = block
    for step in range(1, (size - 1) // 2 + 1):
        up = shift(up, axis, 1)
        down = shift(down, axis, -1)
        found[size - step] = up
        found[step] = down
    if size % 2 == 0 and size > 1:
        half = block.shape[1] // 2
        left = shift(up[:, :half], axis, 1)
        right = shift(down[:, half:], axis, -1)
        found[size // 2] = jnp.concatenate([left, right], axis=1)
    return [found[k] for k in range(size)]


def scatter_sum(parts, axis):
    size = lax.axis_size(axis)
    bits = []
    bit = 1
    while bit < size:
        bits.append(bit)
        bit *= 2
    sent = jnp.stack([parts[p].astype(jnp.bfloat16) for p in range(size) if p & 1])
    got = swap(sent, axis, 1)
    kept = [parts[p] + got[i] for i, p in enumerate(range(0, size, 2))]
    half = kept[0].shape[1] // 2
    done = []
    for side, order in ((0, bits[1:]), (1, bits[1:][::-1])):
        live = {
            p: kept[p // 2][:, side * half : (side + 1) * half] for p in range(0, size, 2)
        }
        for bit in order:
            stay = [p for p in live if not p & bit]
            sent = jnp.stack([live[p ^ bit].astype(jnp.bfloat16) for p in stay])
            got = swap(sent, axis, bit)
            live = {p: live[p] + got[i] for i, p in enumerate(stay)}
        done.append(live[0])
    return jnp.concatenate(done, axis=1)


def shards(inputs, grad_out, w_base, adapter_down_matrix, b_factor):
    width_in = w_base.shape[0]
    owner_rows = inputs.shape[0]
    wide_count = lax.axis_size("wide")
    narrow_count = lax.axis_size("narrow")
    me_wide = lax.axis_index("wide")
    me_narrow = lax.axis_index("narrow")
    token_total_count = owner_rows * wide_count
    adapter_matrix = adapter_scale / token_total_count
    share = grad_out.shape[0] // owner_rows

    starts = list(range(0, owner_rows, piece_rows))
    rows_of = [min(piece_rows, owner_rows - s) for s in starts]
    own = grad_out.reshape(share, owner_rows, grad_out.shape[1])
    gathered = []
    for s, r in zip(starts, rows_of):
        block = own[:, s : s + r].reshape(share * r, -1)
        if len(gathered) > 1:
            block, *earlier = lax.optimization_barrier([block] + gathered[-2])
            gathered[-2] = earlier
        gathered.append(ring_gather(block, "narrow"))

    low_rank_gradient = sum_over(contract_trailing_axis(grad_out, b_factor), "wide").astype(jnp.bfloat16)
    low_rank_all = gather_over(low_rank_gradient, "narrow")
    low_rank_own = lax.dynamic_slice_in_dim(low_rank_all, me_wide * owner_rows, owner_rows)
    low_term = adapter_scale * contract_trailing_axis(low_rank_own, adapter_down_matrix)

    low_act = sum_over(
        jnp.dot(inputs, adapter_down_matrix, preferred_element_type=jnp.float32), "narrow"
    ).astype(jnp.bfloat16)
    low_act_all = gather_over(low_act, "wide")
    low_act_ring = jnp.roll(
        low_act_all.reshape(narrow_count, share, owner_rows, -1), -me_narrow, axis=0
    )

    columns = lax.all_to_all(inputs, "wide", split_axis=1, concat_axis=0, tiled=True)
    grad_a = lax.all_gather(
        adapter_matrix * contract_first(columns, low_rank_all), "wide", axis=0, tiled=True
    )

    grad_b = None
    results = []
    for s, r, blocks in zip(starts, rows_of, gathered):
        tokens = jnp.concatenate(blocks, axis=0)
        part = contract_trailing_axis(tokens, w_base).reshape(narrow_count, share, r, width_in)
        parts = []
        for p in range(wide_count):
            owner = me_wide ^ p
            distance = (owner // share - me_narrow) % narrow_count
            picked = lax.dynamic_slice(
                part, (distance, owner % share, 0, 0), (1, 1, r, width_in)
            )
            parts.append(picked.reshape(r, width_in))
        summed = scatter_sum(parts, "wide")
        results.append((summed + low_term[s : s + r]).astype(jnp.bfloat16))
        acts = low_act_ring[:, :, s : s + r].reshape(narrow_count * share * r, -1)
        term = contract_first(acts, tokens)
        grad_b = term if grad_b is None else grad_b + term
    input_gradient = jnp.concatenate(results, axis=0)
    return (input_gradient, grad_a, adapter_matrix * grad_b)


def solution(mesh):
    return jax.shard_map(
        shards,
        mesh=mesh,
        in_specs=(
            P("wide", "narrow"),
            P("narrow", "wide"),
            P("narrow", "wide"),
            P("narrow", None),
            P(None, "wide"),
        ),
        out_specs=(P("wide", "narrow"), P("narrow", None), P(None, "wide")),
        check_vma=False,
    )
```

```python
import functools

import jax
import jax.numpy as jnp
from jax import lax
from jax.experimental import pallas as pl
from jax.experimental.pallas import tpu as pltpu
from jax.sharding import PartitionSpec as P

adapter_scale = 2.0
piece_rows = 32
weight_rows = 256
vmem_bytes = 40 * 2**20


def contract_trailing_axis(left, right):
    return lax.dot_general(
        left, right, (((1,), (1,)), ((), ())), preferred_element_type=jnp.float32
    )


def contract_first(left, right):
    return lax.dot_general(
        left, right, (((0,), (0,)), ((), ())), preferred_element_type=jnp.float32
    )


def bits_of(axis):
    size = lax.axis_size(axis)
    return [1 << i for i in range(size.bit_length() - 1)]


def swap(value, axis, bit):
    size = lax.axis_size(axis)
    return lax.ppermute(value, axis, [(i, i ^ bit) for i in range(size)])


def shift(value, axis, by):
    size = lax.axis_size(axis)
    return lax.ppermute(value, axis, [(i, (i + by) % size) for i in range(size)])


def scatter_small(value, axis):
    me = lax.axis_index(axis)
    for bit in reversed(bits_of(axis)):
        pair = value.reshape(2, value.shape[0] // 2, value.shape[1])
        mine = ((me & bit) != 0).astype(jnp.int32)
        kept = lax.dynamic_index_in_dim(pair, mine, 0, keepdims=False)
        sent = lax.dynamic_index_in_dim(pair, 1 - mine, 0, keepdims=False)
        value = kept + swap(sent, axis, bit)
    return value


def scatter_direct(value, axis):
    size = lax.axis_size(axis)
    me = lax.axis_index(axis)
    rows = value.shape[0] // size
    blocks = value.reshape(size, rows, value.shape[1])
    found = [
        swap(lax.dynamic_index_in_dim(blocks, me ^ p, 0, keepdims=False), axis, p)
        for p in range(1, size)
    ]
    return lax.dynamic_index_in_dim(blocks, me, 0, keepdims=False), found


def gather_direct(value, axis):
    return [value] + [swap(value, axis, p) for p in range(1, lax.axis_size(axis))]


def by_index(blocks, axis):
    value = jnp.stack(blocks)
    me = lax.axis_index(axis)
    for bit in bits_of(axis):
        pair = value.reshape(value.shape[0] // (2 * bit), 2, bit, *value.shape[1:])
        value = jnp.where((me & bit) != 0, pair[:, ::-1], pair).reshape(value.shape)
    return value


def gather_relative(value, axis, order):
    value = value[None]
    for bit in order:
        value = jnp.concatenate([value, swap(value, axis, bit)], axis=0)
    return value


def gather_ordered(value, axis, order):
    me = lax.axis_index(axis)
    for bit in order:
        other = swap(value, axis, bit)
        upper = (me & bit) != 0
        value = jnp.concatenate(
            [jnp.where(upper, other, value), jnp.where(upper, value, other)], axis=0
        )
    return value


def first_hops(block, axis):
    size = lax.axis_size(axis)
    if size == 4:
        far = swap(block, axis, 2)
        near = swap(block, axis, 1)
        middle = lax.ppermute(block, axis, [(1, 2), (2, 1)])
        return [far, near, middle]
    return [shift(block, axis, 1), shift(block, axis, -1)]


def last_hops(block, hops, axis):
    size = lax.axis_size(axis)
    me = lax.axis_index(axis)
    if size == 4:
        far, near, middle = hops
        ends = (me == 0) | (me == 3)
        onward = lax.ppermute(far, axis, [(1, 0), (2, 3)])
        return [
            (block, me, True),
            (near, me ^ 1, True),
            (far, me ^ 2, True),
            (middle, me ^ 3, ~ends),
            (onward, me ^ 3, ends),
        ]
    up, down = hops
    found = [(block, me, True)]
    for step in range(1, size):
        if step % 2:
            found.append((up, (me + size - (step + 1) // 2) % size, True))
            if step + 2 < size:
                up = shift(up, axis, 1)
        else:
            found.append((down, (me + step // 2) % size, True))
            if step + 2 < size:
                down = shift(down, axis, -1)
    return found


def pass_kernel(places, *refs, sources, share, rows, final, summed):
    source_refs, refs = refs[:sources], refs[sources:]
    weight, refs = refs[0], refs[1:]
    before, refs = (refs[0], refs[1:]) if summed else (None, refs)
    tokens, outs = refs[0], refs[1:]

    @pl.when(pl.program_id(0) == 0)
    def _():
        for i, source in enumerate(source_refs):
            for h in range(share):
                place = places[i * share + h]

                @pl.when(place >= 0)
                def _():
                    start = pl.multiple_of(place * rows, rows)
                    tokens[pl.ds(start, rows), :] = source[h * rows : (h + 1) * rows, :]

    product = contract_trailing_axis(tokens[...], weight[...])
    if summed:
        product = product + before[...]
    if final:
        half = product.shape[0] // 2
        outs[0][...] = product[:half]
        outs[1][...] = product[half:].astype(jnp.bfloat16)
    else:
        outs[0][...] = product


def weight_pass(places, sources, weight, depth_block, share, rows, owners, final, before=None):
    depth = sources[0].shape[1]
    width = weight.shape[0]
    total = owners * rows
    column = lambda i, *_: (0, i)
    whole = lambda i, *_: (0, 0)
    operands = [*sources, weight]
    in_specs = [pl.BlockSpec(s.shape, whole) for s in sources]
    in_specs.append(pl.BlockSpec((weight_rows, depth), lambda i, *_: (i, depth_block)))
    if before is not None:
        operands.append(before)
        in_specs.append(pl.BlockSpec((total, weight_rows), column))
    out_shape = [jax.ShapeDtypeStruct((total, depth), jnp.bfloat16)]
    out_specs = [pl.BlockSpec((total, depth), whole)]
    if final:
        out_shape += [
            jax.ShapeDtypeStruct((total // 2, width), jnp.float32),
            jax.ShapeDtypeStruct((total // 2, width), jnp.bfloat16),
        ]
        out_specs += [pl.BlockSpec((total // 2, weight_rows), column)] * 2
    else:
        out_shape.append(jax.ShapeDtypeStruct((total, width), jnp.float32))
        out_specs.append(pl.BlockSpec((total, weight_rows), column))
    return pl.pallas_call(
        functools.partial(
            pass_kernel,
            sources=len(sources),
            share=share,
            rows=rows,
            final=final,
            summed=before is not None,
        ),
        grid_spec=pltpu.PrefetchScalarGridSpec(
            num_scalar_prefetch=1,
            grid=(width // weight_rows,),
            in_specs=in_specs,
            out_specs=out_specs,
        ),
        out_shape=out_shape,
        compiler_params=pltpu.CompilerParams(vmem_limit_bytes=vmem_bytes),
        cost_estimate=pl.CostEstimate(
            flops=2 * total * depth * width,
            bytes_accessed=2 * width * depth + 4 * total * depth,
            transcendentals=0,
        ),
        name="weight_pass",
    )(places, *operands)


def scatter_sum(kept, sent, axis, owners, rows):
    bits = bits_of(axis)
    live = (kept + swap(sent, axis, 1)).reshape(owners // 2, rows, -1)
    half = live.shape[2] // 2
    done = []
    for side, order in ((0, bits[:-1]), (1, bits[:-1][::-1])):
        part = {p: live[p, :, side * half : (side + 1) * half] for p in range(owners // 2)}
        for bit in order:
            stay = [p for p in part if not p & bit]
            away = jnp.stack([part[p ^ bit].astype(jnp.bfloat16) for p in stay])
            got = swap(away, axis, 2 * bit)
            part = {p: part[p] + got[i] for i, p in enumerate(stay)}
        done.append(part[0])
    return done


def hold(*groups):
    leaves, tree = jax.tree.flatten(groups)
    return jax.tree.unflatten(tree, lax.optimization_barrier(leaves))


def cut_rows(owner_rows, depth):
    sizes = []
    left = owner_rows
    while left:
        sizes.insert(0, min(left, piece_rows))
        left -= sizes[0]
    if len(sizes) > 2 and sizes[0] < piece_rows:
        sizes = [sizes[0] + sizes[1], *sizes[2:]]
    cuts = max(c for c in (4, 2, 1) if depth % (c * 128) == 0)
    tail = depth // cuts
    pieces = []
    start = 0
    for rows in sizes:
        pieces.append((start, rows, 0, depth))
        start += rows
    if cuts > 1:
        start, rows, _, _ = pieces.pop()
        pieces += [(start, rows, 0, depth - tail), (start, rows, depth - tail, depth)]
    return pieces


def shards(inputs, grad_out, w_base, adapter_down_matrix, b_factor):
    owner_rows = inputs.shape[0]
    owners = lax.axis_size("wide")
    me_wide = lax.axis_index("wide")
    adapter_matrix = adapter_scale / (owner_rows * owners)
    share = grad_out.shape[0] // owner_rows
    rank = b_factor.shape[0]
    depth = grad_out.shape[1]
    wide_bits = bits_of("wide")
    pieces = cut_rows(owner_rows, depth)
    count = len(pieces)

    def block_of(source, piece):
        start, rows, low, high = piece
        own = source.reshape(share, owner_rows, depth)
        return own[:, start : start + rows, low:high].reshape(share * rows, high - low)

    blocks = {0: block_of(grad_out, pieces[0])}
    hops = {0: first_hops(blocks[0], "narrow")}

    act_own, act_others = scatter_direct(
        jnp.dot(inputs, adapter_down_matrix, preferred_element_type=jnp.float32), "narrow"
    )
    low_small = scatter_small(contract_trailing_axis(grad_out, b_factor), "wide").astype(jnp.bfloat16)
    grad_out, low_small = hold(grad_out, low_small)
    low_blocks = gather_direct(low_small, "narrow")
    blocks[1] = block_of(grad_out, pieces[1])
    hops[1] = first_hops(blocks[1], "narrow")

    hops[0], act_own, act_others, low_blocks, grad_out, inputs = hold(
        hops[0], act_own, act_others, low_blocks, grad_out, inputs
    )
    found = {0: last_hops(blocks[0], hops[0], "narrow")}
    places = []
    for _, block, valid in found[0]:
        for h in range(share):
            p = (block * share + h) ^ me_wide
            place = (p & 1) * (owners // 2) + (p >> 1)
            places.append(jnp.where(valid, place, -1).astype(jnp.int32))
    places = jnp.stack(places)
    found[0] = [array for array, _, _ in found[0]]
    blocks[2] = block_of(grad_out, pieces[2])
    hops[2] = first_hops(blocks[2], "narrow")
    act_blocks = gather_direct((act_own + sum(act_others)).astype(jnp.bfloat16), "narrow")

    low_wide = gather_ordered(by_index(low_blocks, "narrow")[None], "wide", wide_bits)
    low_rank_all = jnp.swapaxes(low_wide, 0, 1).reshape(owner_rows * owners, rank)
    low_rank_own = lax.dynamic_slice_in_dim(low_rank_all, me_wide * owner_rows, owner_rows)
    low_term = adapter_scale * contract_trailing_axis(low_rank_own, adapter_down_matrix)
    shares = inputs.reshape(owner_rows, owners, -1)
    flipped = [
        sum(bit for i, bit in enumerate(wide_bits) if w & wide_bits[len(wide_bits) - 1 - i])
        for w in range(owners)
    ]
    columns = lax.all_to_all(
        jnp.stack([shares[:, f] for f in flipped], axis=0), "wide", split_axis=0, concat_axis=0
    ).reshape(owner_rows * owners, -1)
    grad_a = adapter_matrix * contract_first(columns, low_rank_all)
    grad_a_steps = wide_bits[::-1]

    sums, tokens, grad_b, results = {}, {}, None, {}
    acts = None

    def run_pass(i):
        _, rows, low, high = pieces[i]
        final = high == depth
        before = None if low == 0 else sums.pop(i - 1)[0]
        tokens[i], *sums[i] = weight_pass(
            places, found[i], w_base, low // (high - low), share, rows, owners, final, before
        )

    def finish(i, acc):
        start, rows, low, _ = pieces[i]
        held = tokens[i] if low == 0 else jnp.concatenate([tokens[i - 1], tokens[i]], axis=1)
        piece_acts = acts[:, start : start + rows].reshape(owners * rows, rank)
        term = contract_first(piece_acts, held)
        acc = term if acc is None else acc + term
        sides = scatter_sum(*sums.pop(i), "wide", owners, rows)
        half = sides[0].shape[1]
        mine = low_term[start : start + rows]
        results[i] = jnp.concatenate(
            [
                (side + mine[:, j * half : (j + 1) * half]).astype(jnp.bfloat16)
                for j, side in enumerate(sides)
            ],
            axis=1,
        )
        return acc

    for i in range(1, count):
        hops[i], found[i - 1], grad_out, grad_a, act_blocks, sums, grad_b, results, acts, low_term = hold(
            hops[i], found[i - 1], grad_out, grad_a, act_blocks, sums, grad_b, results, acts, low_term
        )
        found[i] = [array for array, _, _ in last_hops(blocks[i], hops[i], "narrow")]
        if i + 2 < count:
            blocks[i + 2] = block_of(grad_out, pieces[i + 2])
            hops[i + 2] = first_hops(blocks[i + 2], "narrow")
        if i >= 2 and pieces[i - 2][3] == depth:
            grad_b = finish(i - 2, grad_b)
        run_pass(i - 1)
        if acts is None:
            act_rows = by_index(act_blocks, "narrow").reshape(owner_rows, rank)
            acts = gather_relative(act_rows, "wide", wide_bits[1:] + wide_bits[:1])
        if grad_a_steps:
            grad_a = gather_ordered(grad_a, "wide", grad_a_steps[:1])
            grad_a_steps = grad_a_steps[1:]
    grad_a = gather_ordered(grad_a, "wide", grad_a_steps)
    found[count - 1], sums, grad_b, results, grad_a = hold(
        found[count - 1], sums, grad_b, results, grad_a
    )
    for i in range(count - 2, count - 1):
        if pieces[i][3] == depth:
            grad_b = finish(i, grad_b)
    run_pass(count - 1)
    grad_b = adapter_matrix * finish(count - 1, grad_b)
    return (jnp.concatenate([results[i] for i in sorted(results)], axis=0), grad_a, grad_b)


def solution(mesh):
    return jax.shard_map(
        shards,
        mesh=mesh,
        in_specs=(
            P("wide", "narrow"),
            P("narrow", "wide"),
            P("narrow", "wide"),
            P("narrow", None),
            P(None, "wide"),
        ),
        out_specs=(P("wide", "narrow"), P("narrow", None), P(None, "wide")),
        check_vma=False,
    )
```

```python
import functools

import jax
import jax.numpy as jnp
from jax import lax
from jax.experimental import pallas as pl
from jax.experimental.pallas import tpu as pltpu
from jax.sharding import PartitionSpec as P

adapter_scale = 2.0
piece_rows = 32
weight_rows = 512
vmem_bytes = 40 * 2**20
light = pl.CostEstimate(flops=0, bytes_accessed=2**16, transcendentals=0)


def contract_trailing_axis(left, right):
    return lax.dot_general(
        left, right, (((1,), (1,)), ((), ())), preferred_element_type=jnp.float32
    )


def contract_first(left, right):
    return lax.dot_general(
        left, right, (((0,), (0,)), ((), ())), preferred_element_type=jnp.float32
    )


def bits_of(axis):
    size = lax.axis_size(axis)
    return [1 << i for i in range(size.bit_length() - 1)]


def swap(value, axis, bit):
    size = lax.axis_size(axis)
    return lax.ppermute(value, axis, [(i, i ^ bit) for i in range(size)])


def scatter_small(value, axis):
    me = lax.axis_index(axis)
    for bit in reversed(bits_of(axis)):
        pair = value.reshape(2, value.shape[0] // 2, value.shape[1])
        mine = ((me & bit) != 0).astype(jnp.int32)
        kept = lax.dynamic_index_in_dim(pair, mine, 0, keepdims=False)
        sent = lax.dynamic_index_in_dim(pair, 1 - mine, 0, keepdims=False)
        value = kept + swap(sent, axis, bit)
    return value


def scatter_direct(value, axis):
    size = lax.axis_size(axis)
    me = lax.axis_index(axis)
    rows = value.shape[0] // size
    blocks = value.reshape(size, rows, value.shape[1])
    found = [
        swap(lax.dynamic_index_in_dim(blocks, me ^ p, 0, keepdims=False), axis, p)
        for p in range(1, size)
    ]
    return lax.dynamic_index_in_dim(blocks, me, 0, keepdims=False), found


def gather_direct(value, axis):
    return [value] + [swap(value, axis, p) for p in range(1, lax.axis_size(axis))]


def by_index(blocks, axis):
    value = jnp.stack(blocks)
    me = lax.axis_index(axis)
    for bit in bits_of(axis):
        pair = value.reshape(value.shape[0] // (2 * bit), 2, bit, *value.shape[1:])
        value = jnp.where((me & bit) != 0, pair[:, ::-1], pair).reshape(value.shape)
    return value


def gather_relative(value, axis, order):
    value = value[None]
    for bit in order:
        value = jnp.concatenate([value, swap(value, axis, bit)], axis=0)
    return value


def gather_ordered(value, axis, order):
    me = lax.axis_index(axis)
    for bit in order:
        other = swap(value, axis, bit)
        upper = (me & bit) != 0
        value = jnp.concatenate(
            [jnp.where(upper, other, value), jnp.where(upper, value, other)], axis=0
        )
    return value


def pass_kernel(me, tokens, weight, *refs, owners, rows, final, summed):
    product = contract_trailing_axis(tokens[...], weight[...])
    if summed:
        product = product + refs[0][...]
        refs = refs[1:]
    if not final:
        refs[0][...] = product
        return
    kept, sent = refs
    for core in range(2):

        @pl.when((me[0] & 1) == core)
        def _():
            for owner in range(owners):
                place = (owner ^ me[0]) >> 1
                part = product[owner * rows : (owner + 1) * rows]
                if owner % 2 == core:
                    kept[place] = part
                else:
                    sent[place] = part.astype(jnp.bfloat16)


def weight_pass(me, tokens, weight, depth_block, owners, final, before=None):
    total, depth = tokens.shape
    width = weight.shape[0]
    rows = total // owners
    step = min(weight_rows, width)
    column = lambda i, *_: (0, i)
    operands = [tokens, weight]
    in_specs = [
        pl.BlockSpec((total, depth), lambda i, *_: (0, 0), pipeline_mode=pl.Buffered(1)),
        pl.BlockSpec((step, depth), lambda i, *_: (i, depth_block)),
    ]
    if before is not None:
        operands.append(before)
        in_specs.append(pl.BlockSpec((total, step), column))
    if final:
        half = (owners // 2, rows, width)
        out_shape = [
            jax.ShapeDtypeStruct(half, jnp.float32),
            jax.ShapeDtypeStruct(half, jnp.bfloat16),
        ]
        out_specs = [pl.BlockSpec((owners // 2, rows, step), lambda i, *_: (0, 0, i))] * 2
    else:
        out_shape = [jax.ShapeDtypeStruct((total, width), jnp.float32)]
        out_specs = [pl.BlockSpec((total, step), column)]
    return pl.pallas_call(
        functools.partial(
            pass_kernel, owners=owners, rows=rows, final=final, summed=before is not None
        ),
        grid_spec=pltpu.PrefetchScalarGridSpec(
            num_scalar_prefetch=1,
            grid=(width // step,),
            in_specs=in_specs,
            out_specs=out_specs,
        ),
        out_shape=out_shape,
        compiler_params=pltpu.CompilerParams(vmem_limit_bytes=vmem_bytes),
        cost_estimate=light,
        name="weight_pass",
    )(me, *operands)


def factor_kernel(*refs, count, scale):
    acts, tokens, out = refs[:count], refs[count : 2 * count], refs[-1]
    out[...] = scale * sum(
        jnp.dot(a[...], t[...], preferred_element_type=jnp.float32) for a, t in zip(acts, tokens)
    )


def factor_gradient(acts, tokens, places, scale, depth, step, first, blocks, into=None):
    rank = acts[0].shape[0]
    whole = lambda i: (0, 0)
    in_specs = [pl.BlockSpec(a.shape, whole, pipeline_mode=pl.Buffered(1)) for a in acts]
    in_specs += [
        pl.BlockSpec((t.shape[0], step), lambda i, place=place: (0, first + i - place))
        for t, place in zip(tokens, places)
    ]
    operands = [*acts, *tokens]
    aliases = {}
    if into is not None:
        aliases = {len(operands): 0}
        operands.append(into)
        in_specs.append(pl.BlockSpec(memory_space=pl.ANY))
    return pl.pallas_call(
        functools.partial(factor_kernel, count=len(acts), scale=scale),
        grid=(blocks,),
        in_specs=in_specs,
        out_specs=pl.BlockSpec((rank, step), lambda i: (0, first + i)),
        out_shape=jax.ShapeDtypeStruct((rank, depth), jnp.float32),
        input_output_aliases=aliases,
        compiler_params=pltpu.CompilerParams(vmem_limit_bytes=vmem_bytes),
        cost_estimate=light,
        name="factor_gradient",
    )(*operands)


def scatter_sum(kept, sent, axis):
    bits = bits_of(axis)
    live = kept + swap(sent, axis, 1)
    half = live.shape[2] // 2
    done = []
    for side, order in ((0, bits[:-1]), (1, bits[:-1][::-1])):
        part = {p: live[p, :, side * half : (side + 1) * half] for p in range(live.shape[0])}
        for bit in order:
            stay = [p for p in part if not p & bit]
            away = jnp.stack([part[p ^ bit].astype(jnp.bfloat16) for p in stay])
            got = swap(away, axis, 2 * bit)
            part = {p: part[p] + got[i] for i, p in enumerate(stay)}
        done.append(part[0])
    return done


def hold(*groups):
    leaves, tree = jax.tree.flatten(groups)
    return jax.tree.unflatten(tree, lax.optimization_barrier(leaves))


def cut_rows(owner_rows, depth):
    sizes = []
    left = owner_rows
    while left:
        sizes.insert(0, min(left, piece_rows))
        left -= sizes[0]
    if len(sizes) > 2 and sizes[0] < piece_rows:
        sizes = [sizes[0] + sizes[1], *sizes[2:]]
    cuts = max(c for c in (4, 2, 1) if depth % (c * 128) == 0)
    tail = depth // cuts
    pieces = []
    start = 0
    for rows in sizes:
        pieces.append((start, rows, 0, depth))
        start += rows
    if cuts > 1:
        start, rows, _, _ = pieces.pop()
        pieces += [(start, rows, 0, depth - tail), (start, rows, depth - tail, depth)]
    return pieces


def shards(inputs, grad_out, w_base, adapter_down_matrix, b_factor):
    owner_rows = inputs.shape[0]
    owners = lax.axis_size("wide")
    me_wide = lax.axis_index("wide")
    adapter_matrix = adapter_scale / (owner_rows * owners)
    share = grad_out.shape[0] // owner_rows
    rank = b_factor.shape[0]
    depth = grad_out.shape[1]
    wide_bits = bits_of("wide")
    pieces = cut_rows(owner_rows, depth)
    count = len(pieces)
    me = me_wide.astype(jnp.int32).reshape(1)

    def gather(source, piece):
        start, rows, low, high = piece
        own = source.reshape(share, owner_rows, depth)
        block = own[:, start : start + rows, low:high].reshape(share * rows, high - low)
        return lax.all_gather(block, "narrow", axis=0, tiled=True)

    tokens = {0: gather(grad_out, pieces[0])}

    act_own, act_others = scatter_direct(
        jnp.dot(inputs, adapter_down_matrix, preferred_element_type=jnp.float32), "narrow"
    )
    low_small = scatter_small(contract_trailing_axis(grad_out, b_factor), "wide").astype(jnp.bfloat16)
    low_small, act_own, act_others, grad_out = hold(low_small, act_own, act_others, grad_out)
    for i in range(1, count):
        tokens[i] = gather(grad_out, pieces[i])
    low_blocks = gather_direct(low_small, "narrow")
    act_blocks = gather_direct((act_own + sum(act_others)).astype(jnp.bfloat16), "narrow")

    low_wide = gather_ordered(by_index(low_blocks, "narrow")[None], "wide", wide_bits)
    low_rank_all = jnp.swapaxes(low_wide, 0, 1).reshape(owner_rows * owners, rank)
    low_rank_own = lax.dynamic_slice_in_dim(low_rank_all, me_wide * owner_rows, owner_rows)
    low_term = adapter_scale * contract_trailing_axis(low_rank_own, adapter_down_matrix)
    shares = inputs.reshape(owner_rows, owners, -1)
    flipped = [
        sum(bit for i, bit in enumerate(wide_bits) if w & wide_bits[len(wide_bits) - 1 - i])
        for w in range(owners)
    ]
    columns = lax.all_to_all(
        jnp.stack([shares[:, f] for f in flipped], axis=0), "wide", split_axis=0, concat_axis=0
    ).reshape(owner_rows * owners, -1)
    grad_a = adapter_matrix * contract_first(columns, low_rank_all)
    grad_a_steps = wide_bits[::-1]

    act_rows = by_index(act_blocks, "narrow").reshape(owner_rows, rank)
    acts = gather_ordered(act_rows[None], "wide", wide_bits)
    turned = []
    for start, rows, _, _ in pieces:
        turned.append(acts[:, start : start + rows].reshape(owners * rows, rank).T)

    sums, results, grad_b = {}, {}, None
    tail = pieces[-1][3] - pieces[-1][2]

    def run_pass(i):
        _, _, low, high = pieces[i]
        final = high == depth
        before = None if low == 0 else sums.pop(i - 1)[0]
        sums[i] = weight_pass(me, tokens[i], w_base, low // (high - low), owners, final, before)

    def finish(i):
        start, rows, _, _ = pieces[i]
        sides = scatter_sum(*sums.pop(i), "wide")
        half = sides[0].shape[1]
        mine = low_term[start : start + rows]
        results[i] = jnp.concatenate(
            [
                (side + mine[:, j * half : (j + 1) * half]).astype(jnp.bfloat16)
                for j, side in enumerate(sides)
            ],
            axis=1,
        )

    def factor(low, high, into):
        used = [i for i, piece in enumerate(pieces) if piece[2] <= low and piece[3] >= high]
        return factor_gradient(
            [turned[i] for i in used],
            [tokens[i] for i in used],
            [pieces[i][2] // tail for i in used],
            adapter_matrix,
            depth,
            tail,
            low // tail,
            (high - low) // tail,
            into,
        )

    for i in range(count):
        tokens[i], grad_a, turned, sums, grad_b, results, low_term = hold(
            tokens[i], grad_a, turned, sums, grad_b, results, low_term
        )
        if i and pieces[i - 1][3] == depth:
            finish(i - 1)
        run_pass(i)
        if i == count - 2 and tail < depth:
            grad_b = factor(0, depth - tail, None)
        if grad_a_steps:
            grad_a = gather_ordered(grad_a, "wide", grad_a_steps[:1])
            grad_a_steps = grad_a_steps[1:]
    grad_a = gather_ordered(grad_a, "wide", grad_a_steps)
    grad_b = factor(depth - tail, depth, grad_b)
    finish(count - 1)
    return (jnp.concatenate([results[i] for i in sorted(results)], axis=0), grad_a, grad_b)


def solution(mesh):
    return jax.shard_map(
        shards,
        mesh=mesh,
        in_specs=(
            P("wide", "narrow"),
            P("narrow", "wide"),
            P("narrow", "wide"),
            P("narrow", None),
            P(None, "wide"),
        ),
        out_specs=(P("wide", "narrow"), P("narrow", None), P(None, "wide")),
        check_vma=False,
    )
```

```python
import functools

import jax
import jax.numpy as jnp
from jax import lax
from jax.experimental import pallas as pl
from jax.experimental.pallas import tpu as pltpu
from jax.sharding import PartitionSpec as P

adapter_scale = 2.0
short_rows = 16
weight_rows = 512
vmem_bytes = 40 * 2**20
light = pl.CostEstimate(flops=0, bytes_accessed=2**16, transcendentals=0)


def contract_trailing_axis(left, right):
    return lax.dot_general(
        left, right, (((1,), (1,)), ((), ())), preferred_element_type=jnp.float32
    )


def contract_first(left, right):
    return lax.dot_general(
        left, right, (((0,), (0,)), ((), ())), preferred_element_type=jnp.float32
    )


def bits_of(axis):
    size = lax.axis_size(axis)
    return [1 << i for i in range(size.bit_length() - 1)]


def swap(value, axis, bit):
    size = lax.axis_size(axis)
    return lax.ppermute(value, axis, [(i, i ^ bit) for i in range(size)])


def scatter_small(value, axis):
    me = lax.axis_index(axis)
    for bit in reversed(bits_of(axis)):
        pair = value.reshape(2, value.shape[0] // 2, value.shape[1])
        mine = ((me & bit) != 0).astype(jnp.int32)
        kept = lax.dynamic_index_in_dim(pair, mine, 0, keepdims=False)
        sent = lax.dynamic_index_in_dim(pair, 1 - mine, 0, keepdims=False)
        value = kept + swap(sent, axis, bit)
    return value


def gather_ordered(value, axis, order):
    me = lax.axis_index(axis)
    for bit in order:
        other = swap(value, axis, bit)
        upper = (me & bit) != 0
        value = jnp.concatenate(
            [jnp.where(upper, other, value), jnp.where(upper, value, other)], axis=0
        )
    return value


def phase_a(block, axis):
    return swap(block, axis, 1), swap(block, axis, 2)


def phase_b(block, far, axis):
    return (
        lax.ppermute(block, axis, [(1, 2), (2, 1)]),
        lax.ppermute(far, axis, [(1, 0), (2, 3)]),
    )


def pass_kernel(table, *refs, sources, owners, rows):
    source_refs, refs = refs[:sources], refs[sources:]
    weight, refs = refs[0], refs[1:]
    if sources > 1:
        tokens, kept, sent = refs

        @pl.when(pl.program_id(0) == 0)
        def _():
            size = source_refs[0].shape[0]
            for i, source in enumerate(source_refs[: sources - 2]):
                tokens[i * size : (i + 1) * size] = source[...]
            for end in range(2):

                @pl.when(table[owners] == end)
                def _():
                    tokens[(sources - 2) * size :] = source_refs[sources - 2 + end][...]
    else:
        (tokens,) = source_refs
        kept, sent = refs
    product = contract_trailing_axis(tokens[...], weight[...])
    for i in range(owners):
        place = table[i]
        part = product[i * rows : (i + 1) * rows]

        @pl.when((place & 1) == 0)
        def _():
            kept[place >> 1] = part

        @pl.when((place & 1) == 1)
        def _():
            sent[place >> 1] = part.astype(jnp.bfloat16)


def weight_pass(table, sources, weight, owners):
    depth = weight.shape[1]
    width = weight.shape[0]
    total = sources[0].shape[0] * max(1, len(sources) - 1)
    rows = total // owners
    step = min(weight_rows, width)
    whole = lambda i, *_: (0, 0)
    once = pl.Buffered(1)
    in_specs = [pl.BlockSpec(s.shape, whole, pipeline_mode=once) for s in sources]
    in_specs.append(pl.BlockSpec((step, depth), lambda i, *_: (i, 0)))
    half = (owners // 2, rows, width)
    out_shape = [
        jax.ShapeDtypeStruct(half, jnp.float32),
        jax.ShapeDtypeStruct(half, jnp.bfloat16),
    ]
    out_specs = [pl.BlockSpec((owners // 2, rows, step), lambda i, *_: (0, 0, i))] * 2
    if len(sources) > 1:
        out_shape.insert(0, jax.ShapeDtypeStruct((total, depth), jnp.bfloat16))
        out_specs.insert(0, pl.BlockSpec((total, depth), whole, pipeline_mode=once))
    outs = pl.pallas_call(
        functools.partial(pass_kernel, sources=len(sources), owners=owners, rows=rows),
        grid_spec=pltpu.PrefetchScalarGridSpec(
            num_scalar_prefetch=1,
            grid=(width // step,),
            in_specs=in_specs,
            out_specs=out_specs,
        ),
        out_shape=out_shape,
        compiler_params=pltpu.CompilerParams(vmem_limit_bytes=vmem_bytes),
        cost_estimate=light,
        name="weight_pass",
    )(table, *sources, weight)
    return outs if len(sources) > 1 else [sources[0], *outs]


def factor_kernel(*refs, count, scale):
    acts, tokens, out = refs[:count], refs[count : 2 * count], refs[-1]
    out[...] = scale * sum(
        jnp.dot(a[...], t[...], preferred_element_type=jnp.float32) for a, t in zip(acts, tokens)
    )


def factor_gradient(acts, tokens, scale, step, first, blocks, into=None):
    rank, depth = acts[0].shape[0], tokens[0].shape[1]
    in_specs = [
        pl.BlockSpec(a.shape, lambda i: (0, 0), pipeline_mode=pl.Buffered(1)) for a in acts
    ]
    in_specs += [pl.BlockSpec((t.shape[0], step), lambda i: (0, first + i)) for t in tokens]
    operands = [*acts, *tokens]
    aliases = {}
    if into is not None:
        aliases = {len(operands): 0}
        operands.append(into)
        in_specs.append(pl.BlockSpec(memory_space=pl.ANY))
    return pl.pallas_call(
        functools.partial(factor_kernel, count=len(acts), scale=scale),
        grid=(blocks,),
        in_specs=in_specs,
        out_specs=pl.BlockSpec((rank, step), lambda i: (0, first + i)),
        out_shape=jax.ShapeDtypeStruct((rank, depth), jnp.float32),
        input_output_aliases=aliases,
        compiler_params=pltpu.CompilerParams(vmem_limit_bytes=vmem_bytes),
        cost_estimate=light,
        name="factor_gradient",
    )(*operands)


def scatter_sum(kept, sent, axis):
    bits = bits_of(axis)
    live = kept + swap(sent, axis, 1)
    half = live.shape[2] // 2
    done = []
    for side, order in ((0, bits[:-1]), (1, bits[:-1][::-1])):
        part = {p: live[p, :, side * half : (side + 1) * half] for p in range(live.shape[0])}
        for bit in order:
            stay = [p for p in part if not p & bit]
            away = jnp.stack([part[p ^ bit].astype(jnp.bfloat16) for p in stay])
            got = swap(away, axis, 2 * bit)
            part = {p: part[p] + got[i] for i, p in enumerate(stay)}
        done.append(part[0])
    return done


def hold(*groups):
    leaves, tree = jax.tree.flatten(groups)
    return jax.tree.unflatten(tree, lax.optimization_barrier(leaves))


def cut_rows(owner_rows):
    middle = owner_rows - 2 * short_rows
    sizes = [owner_rows]
    if middle >= 2 * short_rows:
        large = -(-middle * 3 // (5 * short_rows)) * short_rows
        sizes = [short_rows, large, middle - large, short_rows]
    starts = [sum(sizes[:i]) for i in range(len(sizes))]
    return list(zip(starts, sizes))


def shards(inputs, grad_out, w_base, adapter_down_matrix, b_factor):
    owner_rows = inputs.shape[0]
    owners = lax.axis_size("wide")
    groups = lax.axis_size("narrow")
    me_wide = lax.axis_index("wide")
    me_narrow = lax.axis_index("narrow")
    adapter_matrix = adapter_scale / (owner_rows * owners)
    share = grad_out.shape[0] // owner_rows
    rank = b_factor.shape[0]
    depth = grad_out.shape[1]
    wide_bits, narrow_bits = bits_of("wide"), bits_of("narrow")
    pieces = cut_rows(owner_rows)
    count = len(pieces)
    line = groups == 4

    held = [me_narrow ^ i if line else jnp.int32(i) for i in range(groups)]
    table = [(block * share + h) ^ me_wide for block in held for h in range(share)]
    table.append(((me_narrow == 0) | (me_narrow == groups - 1)).astype(jnp.int32))
    table = jnp.stack([entry.astype(jnp.int32) for entry in table])

    def block_of(source, i):
        start, rows = pieces[i]
        own = source.reshape(share, owner_rows, depth)
        return own[:, start : start + rows].reshape(share * rows, depth)

    blocks, near, far, middle, onward = {}, {}, {}, {}, {}

    def begin(i):
        blocks[i] = block_of(grad_out, i)
        if line:
            near[i], far[i] = phase_a(blocks[i], "narrow")
        else:
            near[i] = far[i] = lax.all_gather(blocks[i], "narrow", axis=0, tiled=True)

    def complete(i):
        if line:
            middle[i], onward[i] = phase_b(blocks[i], far[i], "narrow")
        else:
            middle[i], onward[i] = near[i], far[i]

    begin(0)

    act_part = jnp.dot(inputs, adapter_down_matrix, preferred_element_type=jnp.float32)
    act_small = scatter_small(act_part, "narrow").astype(jnp.bfloat16)
    low_part = contract_trailing_axis(grad_out, b_factor)
    low_small = scatter_small(low_part, "wide").astype(jnp.bfloat16)
    near[0], far[0], grad_out, low_small = hold(near[0], far[0], grad_out, low_small)
    complete(0)
    act_rows = gather_ordered(act_small, "narrow", narrow_bits)
    low_rows = gather_ordered(low_small[None], "narrow", narrow_bits)
    middle[0], onward[0], grad_out, act_rows, low_rows, inputs = hold(
        middle[0], onward[0], grad_out, act_rows, low_rows, inputs
    )
    if count > 1:
        begin(1)

    low_wide = gather_ordered(low_rows[None], "wide", wide_bits)
    low_rank_all = jnp.swapaxes(low_wide, 0, 1).reshape(owner_rows * owners, rank)
    low_rank_own = lax.dynamic_slice_in_dim(low_rank_all, me_wide * owner_rows, owner_rows)
    low_term = adapter_scale * contract_trailing_axis(low_rank_own, adapter_down_matrix)
    shares = inputs.reshape(owner_rows, owners, -1)
    flipped = [
        sum(bit for i, bit in enumerate(wide_bits) if w & wide_bits[len(wide_bits) - 1 - i])
        for w in range(owners)
    ]
    columns = lax.all_to_all(
        jnp.stack([shares[:, f] for f in flipped], axis=0), "wide", split_axis=0, concat_axis=0
    ).reshape(owner_rows * owners, -1)
    grad_a = adapter_matrix * contract_first(columns, low_rank_all)
    grad_a_steps = wide_bits[::-1]

    acts = gather_ordered(act_rows[None], "wide", wide_bits).reshape(groups, share, owner_rows, rank)
    if line:
        for bit in narrow_bits:
            pair = acts.reshape(groups // (2 * bit), 2, bit, share, owner_rows, rank)
            acts = jnp.where((me_narrow & bit) != 0, pair[:, ::-1], pair).reshape(acts.shape)
    turned = [
        acts[:, :, start : start + rows].reshape(owners * rows, rank).T for start, rows in pieces
    ]

    tokens, sums, results = {}, {}, {}

    def run_pass(i):
        sources = [blocks[i], near[i], far[i], middle[i], onward[i]] if line else [near[i]]
        tokens[i], *sums[i] = weight_pass(table, sources, w_base, owners)

    def finish(i):
        start, rows = pieces[i]
        sides = scatter_sum(*sums.pop(i), "wide")
        half = sides[0].shape[1]
        mine = low_term[start : start + rows]
        results[i] = jnp.concatenate(
            [
                (side + mine[:, j * half : (j + 1) * half]).astype(jnp.bfloat16)
                for j, side in enumerate(sides)
            ],
            axis=1,
        )

    run_pass(0)
    for i in range(1, count):
        near[i], far[i], grad_out, grad_a, turned, sums, low_term, results = hold(
            near[i], far[i], grad_out, grad_a, turned, sums, low_term, results
        )
        complete(i)
        if i + 1 < count:
            begin(i + 1)
            middle[i], onward[i], grad_a, sums, blocks[i + 1] = hold(
                middle[i], onward[i], grad_a, sums, blocks[i + 1]
            )
        else:
            middle[i], onward[i], grad_a, sums = hold(middle[i], onward[i], grad_a, sums)
        finish(i - 1)
        run_pass(i)
        if grad_a_steps:
            grad_a = gather_ordered(grad_a, "wide", grad_a_steps[:1])
            grad_a_steps = grad_a_steps[1:]
    grad_a = gather_ordered(grad_a, "wide", grad_a_steps)
    step = max(128 * c for c in range(1, 14) if depth % (128 * c) == 0)
    steps = depth // step
    turned = [turned[i] for i in range(count)]
    tokens = [tokens[i] for i in range(count)]
    grad_b = factor_gradient(turned, tokens, adapter_matrix, step, 0, steps // 2 or 1)
    if steps > 1:
        grad_b = factor_gradient(
            turned, tokens, adapter_matrix, step, steps // 2, steps - steps // 2, grad_b
        )
    finish(count - 1)
    return (jnp.concatenate([results[i] for i in range(count)], axis=0), grad_a, grad_b)


def solution(mesh):
    return jax.shard_map(
        shards,
        mesh=mesh,
        in_specs=(
            P("wide", "narrow"),
            P("narrow", "wide"),
            P("narrow", "wide"),
            P("narrow", None),
            P(None, "wide"),
        ),
        out_specs=(P("wide", "narrow"), P("narrow", None), P(None, "wide")),
        check_vma=False,
    )
```

```python
import functools

import jax
import jax.numpy as jnp
from jax import lax
from jax.experimental import pallas as pl
from jax.experimental.pallas import tpu as pltpu
from jax.sharding import PartitionSpec as P

adapter_scale = 2.0
piece_rows = 32
weight_rows = 512
vmem_bytes = 40 * 2**20
light = pl.CostEstimate(flops=0, bytes_accessed=2**16, transcendentals=0)


def contract_trailing_axis(left, right):
    return lax.dot_general(
        left, right, (((1,), (1,)), ((), ())), preferred_element_type=jnp.float32
    )


def contract_first(left, right):
    return lax.dot_general(
        left, right, (((0,), (0,)), ((), ())), preferred_element_type=jnp.float32
    )


def bits_of(axis):
    size = lax.axis_size(axis)
    return [1 << i for i in range(size.bit_length() - 1)]


def swap(value, axis, bit):
    size = lax.axis_size(axis)
    return lax.ppermute(value, axis, [(i, i ^ bit) for i in range(size)])


def scatter_small(value, axis):
    me = lax.axis_index(axis)
    for bit in reversed(bits_of(axis)):
        pair = value.reshape(2, value.shape[0] // 2, value.shape[1])
        mine = ((me & bit) != 0).astype(jnp.int32)
        kept = lax.dynamic_index_in_dim(pair, mine, 0, keepdims=False)
        sent = lax.dynamic_index_in_dim(pair, 1 - mine, 0, keepdims=False)
        value = kept + swap(sent, axis, bit)
    return value


def gather_ordered(value, axis, order):
    me = lax.axis_index(axis)
    for bit in order:
        other = swap(value, axis, bit)
        upper = (me & bit) != 0
        value = jnp.concatenate(
            [jnp.where(upper, other, value), jnp.where(upper, value, other)], axis=0
        )
    return value


def phase_a(block, axis):
    return swap(block, axis, 1), swap(block, axis, 2)


def phase_b(block, far, axis):
    return (
        lax.ppermute(block, axis, [(1, 2), (2, 1)]),
        lax.ppermute(far, axis, [(1, 0), (2, 3)]),
    )


def pass_kernel(table, *refs, sources, owners, rows):
    source_refs, refs = refs[:sources], refs[sources:]
    weight, refs = refs[0], refs[1:]
    if sources > 1:
        tokens, kept, sent = refs

        @pl.when(pl.program_id(0) == 0)
        def _():
            size = source_refs[0].shape[0]
            for i, source in enumerate(source_refs[: sources - 2]):
                tokens[i * size : (i + 1) * size] = source[...]
            for end in range(2):

                @pl.when(table[owners] == end)
                def _():
                    tokens[(sources - 2) * size :] = source_refs[sources - 2 + end][...]
    else:
        (tokens,) = source_refs
        kept, sent = refs
    product = contract_trailing_axis(tokens[...], weight[...])
    for i in range(owners):
        place = table[i]
        part = product[i * rows : (i + 1) * rows]

        @pl.when((place & 1) == 0)
        def _():
            kept[place >> 1] = part

        @pl.when((place & 1) == 1)
        def _():
            sent[place >> 1] = part.astype(jnp.bfloat16)


def weight_pass(table, sources, weight, owners):
    depth = weight.shape[1]
    width = weight.shape[0]
    total = sources[0].shape[0] * max(1, len(sources) - 1)
    rows = total // owners
    step = min(weight_rows, width)
    whole = lambda i, *_: (0, 0)
    once = pl.Buffered(1)
    in_specs = [pl.BlockSpec(s.shape, whole, pipeline_mode=once) for s in sources]
    in_specs.append(pl.BlockSpec((step, depth), lambda i, *_: (i, 0)))
    half = (owners // 2, rows, width)
    out_shape = [
        jax.ShapeDtypeStruct(half, jnp.float32),
        jax.ShapeDtypeStruct(half, jnp.bfloat16),
    ]
    out_specs = [pl.BlockSpec((owners // 2, rows, step), lambda i, *_: (0, 0, i))] * 2
    if len(sources) > 1:
        out_shape.insert(0, jax.ShapeDtypeStruct((total, depth), jnp.bfloat16))
        out_specs.insert(0, pl.BlockSpec((total, depth), whole, pipeline_mode=once))
    outs = pl.pallas_call(
        functools.partial(pass_kernel, sources=len(sources), owners=owners, rows=rows),
        grid_spec=pltpu.PrefetchScalarGridSpec(
            num_scalar_prefetch=1,
            grid=(width // step,),
            in_specs=in_specs,
            out_specs=out_specs,
        ),
        out_shape=out_shape,
        compiler_params=pltpu.CompilerParams(vmem_limit_bytes=vmem_bytes),
        cost_estimate=light,
        name="weight_pass",
    )(table, *sources, weight)
    return outs if len(sources) > 1 else [sources[0], *outs]


def factor_kernel(*refs, count, scale):
    acts, tokens, out = refs[:count], refs[count : 2 * count], refs[-1]
    out[...] = scale * sum(
        jnp.dot(a[...], t[...], preferred_element_type=jnp.float32) for a, t in zip(acts, tokens)
    )


def factor_gradient(acts, tokens, scale, step, first, blocks, into=None):
    rank, depth = acts[0].shape[0], tokens[0].shape[1]
    in_specs = [
        pl.BlockSpec(a.shape, lambda i: (0, 0), pipeline_mode=pl.Buffered(1)) for a in acts
    ]
    in_specs += [pl.BlockSpec((t.shape[0], step), lambda i: (0, first + i)) for t in tokens]
    operands = [*acts, *tokens]
    aliases = {}
    if into is not None:
        aliases = {len(operands): 0}
        operands.append(into)
        in_specs.append(pl.BlockSpec(memory_space=pl.ANY))
    return pl.pallas_call(
        functools.partial(factor_kernel, count=len(acts), scale=scale),
        grid=(blocks,),
        in_specs=in_specs,
        out_specs=pl.BlockSpec((rank, step), lambda i: (0, first + i)),
        out_shape=jax.ShapeDtypeStruct((rank, depth), jnp.float32),
        input_output_aliases=aliases,
        compiler_params=pltpu.CompilerParams(vmem_limit_bytes=vmem_bytes),
        cost_estimate=light,
        name="factor_gradient",
    )(*operands)


def scatter_begin(live):
    half = live.shape[2] // 2
    return [
        {p: live[p, :, side * half : (side + 1) * half] for p in range(live.shape[0])}
        for side in range(2)
    ]


def scatter_hop(state, hop):
    if hop == 0:
        kept, sent = state
        return scatter_begin(kept + swap(sent, "wide", 1))
    bits = bits_of("wide")[:-1]
    done = []
    for part, order in zip(state, (bits, bits[::-1])):
        bit = order[hop - 1]
        stay = [p for p in part if not p & bit]
        away = jnp.stack([part[p ^ bit].astype(jnp.bfloat16) for p in stay])
        got = swap(away, "wide", 2 * bit)
        done.append({p: part[p] + got[i] for i, p in enumerate(stay)})
    return done


def hold(*groups):
    leaves, tree = jax.tree.flatten(groups)
    return jax.tree.unflatten(tree, lax.optimization_barrier(leaves))


def cut_rows(owner_rows):
    sizes = [piece_rows] * (owner_rows // piece_rows)
    if not sizes:
        sizes = [owner_rows]
    sizes[0] += owner_rows - sum(sizes)
    starts = [sum(sizes[:i]) for i in range(len(sizes))]
    return list(zip(starts, sizes))


def shards(inputs, grad_out, w_base, adapter_down_matrix, b_factor):
    owner_rows = inputs.shape[0]
    owners = lax.axis_size("wide")
    groups = lax.axis_size("narrow")
    me_wide = lax.axis_index("wide")
    me_narrow = lax.axis_index("narrow")
    adapter_matrix = adapter_scale / (owner_rows * owners)
    share = grad_out.shape[0] // owner_rows
    rank = b_factor.shape[0]
    depth = grad_out.shape[1]
    wide_bits, narrow_bits = bits_of("wide"), bits_of("narrow")
    pieces = cut_rows(owner_rows)
    count = len(pieces)
    line = groups == 4

    held = [me_narrow ^ i if line else jnp.int32(i) for i in range(groups)]
    table = [(block * share + h) ^ me_wide for block in held for h in range(share)]
    table.append(((me_narrow == 0) | (me_narrow == groups - 1)).astype(jnp.int32))
    table = jnp.stack([entry.astype(jnp.int32) for entry in table])

    def block_of(source, i):
        start, rows = pieces[i]
        own = source.reshape(share, owner_rows, depth)
        return own[:, start : start + rows].reshape(share * rows, depth)

    blocks, near, far, middle, onward = {}, {}, {}, {}, {}

    def begin(i):
        if line:
            near[i], far[i] = phase_a(blocks[i], "narrow")
        else:
            near[i] = far[i] = lax.all_gather(blocks[i], "narrow", axis=0, tiled=True)

    def complete(i):
        if line:
            middle[i], onward[i] = phase_b(blocks[i], far[i], "narrow")
        else:
            middle[i], onward[i] = near[i], far[i]

    blocks[0] = block_of(grad_out, 0)
    begin(0)

    act_sum = jnp.dot(inputs, adapter_down_matrix, preferred_element_type=jnp.float32)
    low_part = contract_trailing_axis(grad_out, b_factor)
    low_small = scatter_small(low_part, "wide").astype(jnp.bfloat16)

    def exchange(act_sum, low_rows, bit):
        count, part = low_rows.shape[0], low_rows.shape[1]
        both = jnp.concatenate([act_sum, low_rows.reshape(-1, rank).astype(jnp.float32)], axis=0)
        got = swap(both, "narrow", bit)
        other = got[owner_rows:].reshape(count, part, rank).astype(jnp.bfloat16)
        upper = (me_narrow & bit) != 0
        first, second = jnp.where(upper, other, low_rows), jnp.where(upper, low_rows, other)
        return act_sum + got[:owner_rows], jnp.concatenate([first, second], axis=0)

    low_rows = low_small[None]
    near[0], far[0], blocks[0], grad_out, low_rows, act_sum, inputs = hold(
        near[0], far[0], blocks[0], grad_out, low_rows, act_sum, inputs
    )
    complete(0)
    blocks[1] = block_of(grad_out, 1)
    for bit in narrow_bits:
        act_sum, low_rows = exchange(act_sum, low_rows, bit)
    act_rows = act_sum.astype(jnp.bfloat16)
    small = {"rows": jnp.concatenate([act_rows, low_rows.reshape(-1, rank)], axis=0)[None]}

    def first_hop(bit):
        small["rows"] = gather_ordered(small["rows"], "wide", [bit])

    def regroup():
        shares = small.pop("inputs").reshape(owner_rows, owners, -1)
        flipped = [
            sum(bit for i, bit in enumerate(wide_bits) if w & wide_bits[len(wide_bits) - 1 - i])
            for w in range(owners)
        ]
        shares = jnp.stack([shares[:, f] for f in flipped], axis=0)
        columns = lax.all_to_all(shares, "wide", split_axis=0, concat_axis=0)
        small["columns"] = columns.reshape(owner_rows * owners, -1)

    def share_made():
        rows = small.pop("rows")
        low_wide = rows[:, owner_rows:].reshape(owners, groups, low_small.shape[0], rank)
        low_all = jnp.swapaxes(low_wide, 0, 1).reshape(owner_rows * owners, rank)
        low_own = lax.dynamic_slice_in_dim(low_all, me_wide * owner_rows, owner_rows)
        small["term"] = adapter_scale * contract_trailing_axis(low_own, adapter_down_matrix)
        made = adapter_matrix * contract_first(small.pop("columns"), low_all)
        small["grad_a"] = made.astype(jnp.bfloat16)
        acts = rows[:, :owner_rows].reshape(groups, share, owner_rows, rank)
        if line:
            for bit in narrow_bits:
                cut = acts.reshape(groups // (2 * bit), 2, bit, share, owner_rows, rank)
                acts = jnp.where((me_narrow & bit) != 0, cut[:, ::-1], cut).reshape(acts.shape)
        small["turned"] = [
            acts[:, :, start : start + rows].reshape(owners * rows, rank).T
            for start, rows in pieces
        ]

    def second_hop(bit):
        if "grad_a" not in small:
            share_made()
        small["grad_a"] = gather_ordered(small["grad_a"], "wide", [bit])

    hops = [functools.partial(first_hop, bit) for bit in wide_bits]
    hops += [functools.partial(second_hop, bit) for bit in wide_bits[::-1]]
    small["inputs"] = inputs
    tokens, sums = {}, {}
    waiting = {}

    def step():
        if hops:
            hops.pop(0)()
        for i in sums:
            if waiting[i]:
                sums[i] = scatter_hop(sums[i], waiting[i].pop(0))

    def run_pass(i):
        sources = [blocks[i], near[i], far[i], middle[i], onward[i]] if line else [near[i]]
        tokens[i], kept, sent = weight_pass(table, sources, w_base, owners)
        sums[i] = (kept, sent)
        waiting[i] = list(range(len(wide_bits)))

    for i in range(count):
        if i:
            near[i], far[i], blocks, grad_out, small, sums = hold(
                near[i], far[i], blocks, grad_out, small, sums
            )
            complete(i)
            if i + 1 < count:
                blocks[i + 1] = block_of(grad_out, i + 1)
            step()
        middle[i], onward[i], blocks, grad_out, small, sums = hold(
            middle[i], onward[i], blocks, grad_out, small, sums
        )
        if i + 1 < count:
            begin(i + 1)
            step()
            if i == 0:
                regroup()
            run_pass(i)
    step()
    run_pass(count - 1)
    while hops:
        hops.pop(0)()
    sums[count - 1] = scatter_hop(sums[count - 1], waiting[count - 1].pop(0))
    columns_step = max(128 * c for c in range(1, 14) if depth % (128 * c) == 0)
    steps = depth // columns_step
    early = steps // 2 or 1
    turned = small["turned"]
    tokens = [tokens[i] for i in range(count)]
    grad_b = factor_gradient(turned, tokens, adapter_matrix, columns_step, 0, early)
    sums[count - 1], grad_b = hold(sums[count - 1], grad_b)
    if steps > early:
        grad_b = factor_gradient(
            turned, tokens, adapter_matrix, columns_step, early, steps - early, grad_b
        )
    results = []
    for i, (start, rows) in enumerate(pieces):
        for hop in waiting[i]:
            sums[i] = scatter_hop(sums[i], hop)
        mine = small["term"][start : start + rows]
        summed = jnp.concatenate([part[0] for part in sums[i]], axis=1)
        results.append((summed + mine).astype(jnp.bfloat16))
    grad_a = small["grad_a"].astype(jnp.float32)
    return (jnp.concatenate(results, axis=0), grad_a, grad_b)


def solution(mesh):
    return jax.shard_map(
        shards,
        mesh=mesh,
        in_specs=(
            P("wide", "narrow"),
            P("narrow", "wide"),
            P("narrow", "wide"),
            P("narrow", None),
            P(None, "wide"),
        ),
        out_specs=(P("wide", "narrow"), P("narrow", None), P(None, "wide")),
        check_vma=False,
    )
```

```python
import functools

import jax
import jax.numpy as jnp
from jax import lax
from jax.experimental import pallas as pl
from jax.experimental.pallas import tpu as pltpu
from jax.sharding import PartitionSpec as P

adapter_scale = 2.0
piece_rows = 32
weight_rows = 512
vmem_bytes = 40 * 2**20
light = pl.CostEstimate(flops=0, bytes_accessed=2**16, transcendentals=0)


def contract_trailing_axis(left, right):
    return lax.dot_general(
        left, right, (((1,), (1,)), ((), ())), preferred_element_type=jnp.float32
    )


def contract_first(left, right):
    return lax.dot_general(
        left, right, (((0,), (0,)), ((), ())), preferred_element_type=jnp.float32
    )


def bits_of(axis):
    size = lax.axis_size(axis)
    return [1 << i for i in range(size.bit_length() - 1)]


def swap(value, axis, bit):
    size = lax.axis_size(axis)
    return lax.ppermute(value, axis, [(i, i ^ bit) for i in range(size)])


def scatter_small(value, axis):
    me = lax.axis_index(axis)
    for bit in reversed(bits_of(axis)):
        pair = value.reshape(2, value.shape[0] // 2, value.shape[1])
        mine = ((me & bit) != 0).astype(jnp.int32)
        kept = lax.dynamic_index_in_dim(pair, mine, 0, keepdims=False)
        sent = lax.dynamic_index_in_dim(pair, 1 - mine, 0, keepdims=False)
        value = kept + swap(sent, axis, bit)
    return value


def gather_ordered(value, axis, order):
    me = lax.axis_index(axis)
    for bit in order:
        other = swap(value, axis, bit)
        upper = (me & bit) != 0
        value = jnp.concatenate(
            [jnp.where(upper, other, value), jnp.where(upper, value, other)], axis=0
        )
    return value


def phase_a(block, axis):
    return swap(block, axis, 1), swap(block, axis, 2)


def phase_b(block, far, axis):
    return (
        lax.ppermute(block, axis, [(1, 2), (2, 1)]),
        lax.ppermute(far, axis, [(1, 0), (2, 3)]),
    )


def pass_kernel(table, *refs, sources, owners, rows):
    source_refs, refs = refs[:sources], refs[sources:]
    weight, refs = refs[0], refs[1:]
    if sources > 1:
        tokens, kept, sent = refs

        @pl.when(pl.program_id(0) == 0)
        def _():
            size = source_refs[0].shape[0]
            for i, source in enumerate(source_refs[: sources - 2]):
                tokens[i * size : (i + 1) * size] = source[...]
            for end in range(2):

                @pl.when(table[owners] == end)
                def _():
                    tokens[(sources - 2) * size :] = source_refs[sources - 2 + end][...]
    else:
        (tokens,) = source_refs
        kept, sent = refs
    product = contract_trailing_axis(weight[...], tokens[...]).T
    for i in range(owners):
        place = table[i]
        part = product[i * rows : (i + 1) * rows]

        @pl.when((place & 1) == 0)
        def _():
            kept[place >> 1] = part

        @pl.when((place & 1) == 1)
        def _():
            sent[place >> 1] = part.astype(jnp.bfloat16)


def weight_pass(table, sources, weight, owners):
    depth = weight.shape[1]
    width = weight.shape[0]
    total = sources[0].shape[0] * max(1, len(sources) - 1)
    rows = total // owners
    step = min(weight_rows, width)
    whole = lambda i, *_: (0, 0)
    once = pl.Buffered(1)
    in_specs = [pl.BlockSpec(s.shape, whole, pipeline_mode=once) for s in sources]
    in_specs.append(pl.BlockSpec((step, depth), lambda i, *_: (i, 0)))
    half = (owners // 2, rows, width)
    out_shape = [
        jax.ShapeDtypeStruct(half, jnp.float32),
        jax.ShapeDtypeStruct(half, jnp.bfloat16),
    ]
    out_specs = [pl.BlockSpec((owners // 2, rows, step), lambda i, *_: (0, 0, i))] * 2
    if len(sources) > 1:
        out_shape.insert(0, jax.ShapeDtypeStruct((total, depth), jnp.bfloat16))
        out_specs.insert(0, pl.BlockSpec((total, depth), whole, pipeline_mode=once))
    outs = pl.pallas_call(
        functools.partial(pass_kernel, sources=len(sources), owners=owners, rows=rows),
        grid_spec=pltpu.PrefetchScalarGridSpec(
            num_scalar_prefetch=1,
            grid=(width // step,),
            in_specs=in_specs,
            out_specs=out_specs,
        ),
        out_shape=out_shape,
        compiler_params=pltpu.CompilerParams(vmem_limit_bytes=vmem_bytes),
        cost_estimate=light,
        name="weight_pass",
    )(table, *sources, weight)
    return outs if len(sources) > 1 else [sources[0], *outs]


def factor_kernel(*refs, count, scale):
    acts, tokens, out = refs[:count], refs[count : 2 * count], refs[-1]
    out[...] = scale * sum(
        jnp.dot(a[...], t[...], preferred_element_type=jnp.float32) for a, t in zip(acts, tokens)
    )


def factor_gradient(acts, tokens, scale, step, first, blocks, into=None):
    rank, depth = acts[0].shape[0], tokens[0].shape[1]
    in_specs = [
        pl.BlockSpec(a.shape, lambda i: (0, 0), pipeline_mode=pl.Buffered(1)) for a in acts
    ]
    in_specs += [pl.BlockSpec((t.shape[0], step), lambda i: (0, first + i)) for t in tokens]
    operands = [*acts, *tokens]
    aliases = {}
    if into is not None:
        aliases = {len(operands): 0}
        operands.append(into)
        in_specs.append(pl.BlockSpec(memory_space=pl.ANY))
    return pl.pallas_call(
        functools.partial(factor_kernel, count=len(acts), scale=scale),
        grid=(blocks,),
        in_specs=in_specs,
        out_specs=pl.BlockSpec((rank, step), lambda i: (0, first + i)),
        out_shape=jax.ShapeDtypeStruct((rank, depth), jnp.float32),
        input_output_aliases=aliases,
        compiler_params=pltpu.CompilerParams(vmem_limit_bytes=vmem_bytes),
        cost_estimate=light,
        name="factor_gradient",
    )(*operands)


def scatter_send(state, hop):
    if hop == 0:
        kept, sent = state
        half = kept.shape[2] // 2
        got = [swap(sent[:, :, side * half : (side + 1) * half], "wide", 1) for side in range(2)]
        return kept, got
    bits = bits_of("wide")[:-1]
    stay, got = [], []
    for part, order in zip(state, (bits, bits[::-1])):
        bit = order[hop - 1]
        stay.append({p: part[p] for p in part if not p & bit})
        away = jnp.stack([part[p | bit].astype(jnp.bfloat16) for p in stay[-1]])
        got.append(swap(away, "wide", 2 * bit))
    return stay, got


def scatter_take(flight, hop):
    stay, got = flight
    if hop == 0:
        half = stay.shape[2] // 2
        return [
            {p: stay[p, :, side * half : (side + 1) * half] + got[side][p] for p in range(stay.shape[0])}
            for side in range(2)
        ]
    return [{p: part[p] + new[i] for i, p in enumerate(part)} for part, new in zip(stay, got)]


def hold(*groups):
    leaves, tree = jax.tree.flatten(groups)
    return jax.tree.unflatten(tree, lax.optimization_barrier(leaves))


def cut_rows(owner_rows):
    sizes = [piece_rows] * (owner_rows // piece_rows)
    if not sizes:
        sizes = [owner_rows]
    sizes[0] += owner_rows - sum(sizes)
    starts = [sum(sizes[:i]) for i in range(len(sizes))]
    return list(zip(starts, sizes))


def shards(inputs, grad_out, w_base, adapter_down_matrix, b_factor):
    owner_rows = inputs.shape[0]
    owners = lax.axis_size("wide")
    groups = lax.axis_size("narrow")
    me_wide = lax.axis_index("wide")
    me_narrow = lax.axis_index("narrow")
    adapter_matrix = adapter_scale / (owner_rows * owners)
    share = grad_out.shape[0] // owner_rows
    rank = b_factor.shape[0]
    depth = grad_out.shape[1]
    wide_bits, narrow_bits = bits_of("wide"), bits_of("narrow")
    pieces = cut_rows(owner_rows)
    count = len(pieces)
    line = groups == 4

    held = [me_narrow ^ i if line else jnp.int32(i) for i in range(groups)]
    table = [(block * share + h) ^ me_wide for block in held for h in range(share)]
    table.append(((me_narrow == 0) | (me_narrow == groups - 1)).astype(jnp.int32))
    table = jnp.stack([entry.astype(jnp.int32) for entry in table])

    def block_of(source, i):
        start, rows = pieces[i]
        own = source.reshape(share, owner_rows, depth)
        return own[:, start : start + rows].reshape(share * rows, depth)

    blocks, near, far, middle, onward = {}, {}, {}, {}, {}

    def begin(i):
        if line:
            near[i], far[i] = phase_a(blocks[i], "narrow")
        else:
            near[i] = far[i] = lax.all_gather(blocks[i], "narrow", axis=0, tiled=True)

    def complete(i):
        if line:
            middle[i], onward[i] = phase_b(blocks[i], far[i], "narrow")
        else:
            middle[i], onward[i] = near[i], far[i]

    blocks[0] = block_of(grad_out, 0)
    begin(0)

    blocks[0], low_source = hold(blocks[0], grad_out)
    low_part = contract_trailing_axis(low_source, b_factor)
    low_small = scatter_small(low_part, "wide").astype(jnp.bfloat16)

    def exchange(act_sum, low_rows, bit):
        both = jnp.concatenate([act_sum, low_rows.reshape(-1, rank).astype(jnp.float32)], axis=0)
        return swap(both, "narrow", bit)

    def exchanged(act_sum, low_rows, got, bit):
        other = got[owner_rows:].reshape(low_rows.shape).astype(jnp.bfloat16)
        upper = (me_narrow & bit) != 0
        first, second = jnp.where(upper, other, low_rows), jnp.where(upper, low_rows, other)
        return act_sum + got[:owner_rows], jnp.concatenate([first, second], axis=0)

    low_rows = low_small[None]
    near[0], far[0], blocks[0], grad_out, low_rows, inputs = hold(
        near[0], far[0], blocks[0], grad_out, low_rows, inputs
    )
    act_sum = jnp.dot(inputs, adapter_down_matrix, preferred_element_type=jnp.float32)
    complete(0)
    blocks[1] = block_of(grad_out, 1)
    for bit in narrow_bits[:-1]:
        act_sum, low_rows = exchanged(act_sum, low_rows, exchange(act_sum, low_rows, bit), bit)
    small = {"inputs": inputs, "act": act_sum, "low": low_rows}
    small["got"] = exchange(act_sum, low_rows, narrow_bits[-1])

    def take():
        if "got" in small and "act" in small:
            act, low = exchanged(small.pop("act"), small.pop("low"), small.pop("got"), narrow_bits[-1])
            small["rows"] = jnp.concatenate([act.astype(jnp.bfloat16), low.reshape(-1, rank)], axis=0)[None]
        elif "got" in small:
            upper = (me_wide & taken.pop(0)) != 0
            name = "rows" if "rows" in small else "grad_a"
            mine, other = small[name], small.pop("got")
            first, second = jnp.where(upper, other, mine), jnp.where(upper, mine, other)
            small[name] = jnp.concatenate([first, second], axis=0)

    taken = wide_bits + wide_bits[::-1]
    bits_left = list(taken)

    def small_hop():
        take()
        if not bits_left:
            return
        if len(bits_left) == len(wide_bits):
            share_made()
        small["got"] = swap(small["rows" if "rows" in small else "grad_a"], "wide", bits_left.pop(0))

    def regroup():
        shares = small.pop("inputs").reshape(owner_rows, owners, -1)
        flipped = [
            sum(bit for i, bit in enumerate(wide_bits) if w & wide_bits[len(wide_bits) - 1 - i])
            for w in range(owners)
        ]
        shares = jnp.stack([shares[:, f] for f in flipped], axis=0)
        columns = lax.all_to_all(shares, "wide", split_axis=0, concat_axis=0)
        small["columns"] = columns.reshape(owner_rows * owners, -1)

    def share_made():
        rows = small.pop("rows")
        low_wide = rows[:, owner_rows:].reshape(owners, groups, low_small.shape[0], rank)
        low_all = jnp.swapaxes(low_wide, 0, 1).reshape(owner_rows * owners, rank)
        low_own = lax.dynamic_slice_in_dim(low_all, me_wide * owner_rows, owner_rows)
        small["term"] = adapter_scale * contract_trailing_axis(low_own, adapter_down_matrix)
        made = adapter_matrix * contract_first(small.pop("columns"), low_all)
        small["grad_a"] = made.astype(jnp.bfloat16)
        acts = rows[:, :owner_rows].reshape(groups, share, owner_rows, rank)
        if line:
            for bit in narrow_bits:
                cut = acts.reshape(groups // (2 * bit), 2, bit, share, owner_rows, rank)
                acts = jnp.where((me_narrow & bit) != 0, cut[:, ::-1], cut).reshape(acts.shape)
        small["turned"] = [
            acts[:, :, start : start + rows].reshape(owners * rows, rank).T
            for start, rows in pieces
        ]

    tokens, sums = {}, {}
    done_hops = {}

    def sum_hop(i):
        if done_hops[i]:
            sums[i] = scatter_take(sums[i], done_hops[i] - 1)
        if done_hops[i] < len(wide_bits):
            sums[i] = scatter_send(sums[i], done_hops[i])
        done_hops[i] += 1

    def step():
        small_hop()
        for i in sums:
            if done_hops[i] <= len(wide_bits):
                sum_hop(i)

    def run_pass(i):
        sources = [blocks[i], near[i], far[i], middle[i], onward[i]] if line else [near[i]]
        tokens[i], kept, sent = weight_pass(table, sources, w_base, owners)
        sums[i] = (kept, sent)
        done_hops[i] = 0
        sum_hop(i)

    for i in range(count):
        if i:
            near[i], far[i], blocks, grad_out, small, sums = hold(
                near[i], far[i], blocks, grad_out, small, sums
            )
            complete(i)
            if i + 1 < count:
                blocks[i + 1] = block_of(grad_out, i + 1)
            step()
        middle[i], onward[i], blocks, grad_out, small, sums = hold(
            middle[i], onward[i], blocks, grad_out, small, sums
        )
        if i + 1 < count:
            begin(i + 1)
            step()
            if i + 2 == count:
                regroup()
            run_pass(i)
    step()
    run_pass(count - 1)
    small, sums = hold(small, sums)
    while bits_left or "got" in small:
        small_hop()
    columns_step = max(128 * c for c in range(1, 14) if depth % (128 * c) == 0)
    steps = depth // columns_step
    early = steps // 2 or 1
    turned = small["turned"]
    tokens = [tokens[i] for i in range(count)]
    grad_b = factor_gradient(turned, tokens, adapter_matrix, columns_step, 0, early)
    sum_hop(count - 1)
    sums[count - 1], grad_b = hold(sums[count - 1], grad_b)
    if steps > early:
        grad_b = factor_gradient(
            turned, tokens, adapter_matrix, columns_step, early, steps - early, grad_b
        )
    results = []
    for i, (start, rows) in enumerate(pieces):
        while done_hops[i] <= len(wide_bits):
            sum_hop(i)
        mine = small["term"][start : start + rows]
        summed = jnp.concatenate([part[0] for part in sums[i]], axis=1)
        results.append((summed + mine).astype(jnp.bfloat16))
    grad_a = small["grad_a"].astype(jnp.float32)
    return (jnp.concatenate(results, axis=0), grad_a, grad_b)


def solution(mesh):
    return jax.shard_map(
        shards,
        mesh=mesh,
        in_specs=(
            P("wide", "narrow"),
            P("narrow", "wide"),
            P("narrow", "wide"),
            P("narrow", None),
            P(None, "wide"),
        ),
        out_specs=(P("wide", "narrow"), P("narrow", None), P(None, "wide")),
        check_vma=False,
    )
```

```python
import functools

import jax
import jax.numpy as jnp
from jax import lax
from jax.experimental import pallas as pl
from jax.experimental.pallas import tpu as pltpu
from jax.sharding import PartitionSpec as P

adapter_scale = 2.0
last_rows = 32
weight_rows = 512
vmem_bytes = 40 * 2**20
light = pl.CostEstimate(flops=0, bytes_accessed=2**16, transcendentals=0)


def contract_trailing_axis(left, right):
    return lax.dot_general(
        left, right, (((1,), (1,)), ((), ())), preferred_element_type=jnp.float32
    )


def contract_first(left, right):
    return lax.dot_general(
        left, right, (((0,), (0,)), ((), ())), preferred_element_type=jnp.float32
    )


def bits_of(axis):
    size = lax.axis_size(axis)
    return [1 << i for i in range(size.bit_length() - 1)]


def swap(value, axis, bit):
    size = lax.axis_size(axis)
    return lax.ppermute(value, axis, [(i, i ^ bit) for i in range(size)])


def scatter_small(value, axis):
    me = lax.axis_index(axis)
    for bit in reversed(bits_of(axis)):
        pair = value.reshape(2, value.shape[0] // 2, value.shape[1])
        mine = ((me & bit) != 0).astype(jnp.int32)
        kept = lax.dynamic_index_in_dim(pair, mine, 0, keepdims=False)
        sent = lax.dynamic_index_in_dim(pair, 1 - mine, 0, keepdims=False)
        value = kept + swap(sent, axis, bit)
    return value


def gather_ordered(value, axis, order):
    me = lax.axis_index(axis)
    for bit in order:
        other = swap(value, axis, bit)
        upper = (me & bit) != 0
        value = jnp.concatenate(
            [jnp.where(upper, other, value), jnp.where(upper, value, other)], axis=0
        )
    return value


def pass_kernel(table, tokens, weight, kept, sent, *, owners, rows):
    product = contract_trailing_axis(tokens[...], weight[...])
    for i in range(owners):
        place = table[i]
        part = product[i * rows : (i + 1) * rows]

        @pl.when((place & 1) == 0)
        def _():
            kept[place >> 1] = part

        @pl.when((place & 1) == 1)
        def _():
            sent[place >> 1] = part.astype(jnp.bfloat16)


def weight_pass(table, tokens, weight, owners):
    total, depth = tokens.shape
    width = weight.shape[0]
    rows = total // owners
    step = min(weight_rows, width)
    half = (owners // 2, rows, width)
    return pl.pallas_call(
        functools.partial(pass_kernel, owners=owners, rows=rows),
        grid_spec=pltpu.PrefetchScalarGridSpec(
            num_scalar_prefetch=1,
            grid=(width // step,),
            in_specs=[
                pl.BlockSpec((total, depth), lambda i, *_: (0, 0), pipeline_mode=pl.Buffered(1)),
                pl.BlockSpec((step, depth), lambda i, *_: (i, 0)),
            ],
            out_specs=[pl.BlockSpec((owners // 2, rows, step), lambda i, *_: (0, 0, i))] * 2,
        ),
        out_shape=[
            jax.ShapeDtypeStruct(half, jnp.float32),
            jax.ShapeDtypeStruct(half, jnp.bfloat16),
        ],
        compiler_params=pltpu.CompilerParams(vmem_limit_bytes=vmem_bytes),
        cost_estimate=light,
        name="weight_pass",
    )(table, tokens, weight)


def factor_kernel(*refs, count, scale):
    acts, tokens, out = refs[:count], refs[count : 2 * count], refs[-1]
    out[...] = scale * sum(
        jnp.dot(a[...], t[...], preferred_element_type=jnp.float32) for a, t in zip(acts, tokens)
    )


def factor_gradient(acts, tokens, scale, step, first, blocks, into=None):
    rank, depth = acts[0].shape[0], tokens[0].shape[1]
    in_specs = [
        pl.BlockSpec(a.shape, lambda i: (0, 0), pipeline_mode=pl.Buffered(1)) for a in acts
    ]
    in_specs += [pl.BlockSpec((t.shape[0], step), lambda i: (0, first + i)) for t in tokens]
    operands = [*acts, *tokens]
    aliases = {}
    if into is not None:
        aliases = {len(operands): 0}
        operands.append(into)
        in_specs.append(pl.BlockSpec(memory_space=pl.ANY))
    return pl.pallas_call(
        functools.partial(factor_kernel, count=len(acts), scale=scale),
        grid=(blocks,),
        in_specs=in_specs,
        out_specs=pl.BlockSpec((rank, step), lambda i: (0, first + i)),
        out_shape=jax.ShapeDtypeStruct((rank, depth), jnp.float32),
        input_output_aliases=aliases,
        compiler_params=pltpu.CompilerParams(vmem_limit_bytes=vmem_bytes),
        cost_estimate=light,
        name="factor_gradient",
    )(*operands)


def scatter_send(state, hop, strips):
    if hop == 0:
        kept, sent = state
        width = kept.shape[2] // strips
        return kept, [
            swap(sent[:, :, i * width : (i + 1) * width], "wide", 1) for i in range(strips)
        ]
    bits = bits_of("wide")[:-1]
    stay, got = [], []
    for i, part in enumerate(state):
        bit = (bits, bits[::-1])[i % 2][hop - 1]
        stay.append({p: part[p] for p in part if not p & bit})
        away = jnp.stack([part[p | bit].astype(jnp.bfloat16) for p in stay[-1]])
        got.append(swap(away, "wide", 2 * bit))
    return stay, got


def scatter_take(flight, hop):
    stay, got = flight
    if hop == 0:
        width = stay.shape[2] // len(got)
        return [
            {p: stay[p, :, i * width : (i + 1) * width] + new[p] for p in range(stay.shape[0])}
            for i, new in enumerate(got)
        ]
    return [{p: part[p] + new[i] for i, p in enumerate(part)} for part, new in zip(stay, got)]


def hold(*groups):
    leaves, tree = jax.tree.flatten(groups)
    return jax.tree.unflatten(tree, lax.optimization_barrier(leaves))


def cut_rows(owner_rows):
    last = last_rows if owner_rows >= 2 * last_rows else 0
    sizes = [owner_rows - last] + [last] * (last > 0)
    starts = [sum(sizes[:i]) for i in range(len(sizes))]
    return list(zip(starts, sizes))


def shards(inputs, grad_out, w_base, adapter_down_matrix, b_factor):
    owner_rows = inputs.shape[0]
    owners = lax.axis_size("wide")
    groups = lax.axis_size("narrow")
    me_wide = lax.axis_index("wide")
    adapter_matrix = adapter_scale / (owner_rows * owners)
    share = grad_out.shape[0] // owner_rows
    rank = b_factor.shape[0]
    depth = grad_out.shape[1]
    wide_bits = bits_of("wide")
    pieces = cut_rows(owner_rows)
    count = len(pieces)
    table = jnp.arange(owners, dtype=jnp.int32) ^ me_wide.astype(jnp.int32)

    def gather(source, i):
        start, rows = pieces[i]
        own = source.reshape(share, owner_rows, depth)
        block = own[:, start : start + rows].reshape(share * rows, depth)
        return lax.all_gather(block, "narrow", axis=0, tiled=True)

    tokens = [gather(grad_out, 0)]

    low_part = contract_trailing_axis(grad_out, b_factor)
    low_small = scatter_small(low_part, "wide").astype(jnp.bfloat16)
    low_small, grad_out = hold(low_small, grad_out)
    for i in range(1, count):
        tokens.append(gather(grad_out, i))
    low_rows = gather_ordered(low_small[None], "narrow", bits_of("narrow"))
    act_part = jnp.dot(inputs, adapter_down_matrix, preferred_element_type=jnp.float32)
    act_small = scatter_small(act_part, "narrow").astype(jnp.bfloat16)
    act_rows = gather_ordered(act_small, "narrow", bits_of("narrow"))
    both = jnp.concatenate([act_rows, low_rows.reshape(-1, rank)], axis=0)
    both = gather_ordered(both[None], "wide", wide_bits)
    low_wide = both[:, owner_rows:].reshape(owners, groups, low_small.shape[0], rank)
    low_all = jnp.swapaxes(low_wide, 0, 1).reshape(owner_rows * owners, rank)
    low_own = lax.dynamic_slice_in_dim(low_all, me_wide * owner_rows, owner_rows)
    low_term = adapter_scale * contract_trailing_axis(low_own, adapter_down_matrix)
    turned = [
        both[:, start : start + rows].reshape(owners * rows, rank).T for start, rows in pieces
    ]

    shares = inputs.reshape(owner_rows, owners, -1)
    flipped = [
        sum(bit for i, bit in enumerate(wide_bits) if w & wide_bits[len(wide_bits) - 1 - i])
        for w in range(owners)
    ]
    shares = jnp.stack([shares[:, f] for f in flipped], axis=0)
    columns = lax.all_to_all(shares, "wide", split_axis=0, concat_axis=0)
    columns = columns.reshape(owner_rows * owners, -1)
    grad_a = adapter_matrix * contract_first(columns, low_all)
    grad_a = gather_ordered(grad_a, "wide", wide_bits[::-1])

    columns_step = max(128 * c for c in range(1, 14) if depth % (128 * c) == 0)
    steps = depth // columns_step
    early = steps // 2 or 1

    def hops(state, first, end, strips):
        for hop in range(first, end):
            state = scatter_take(scatter_send(state, hop, strips), hop)
        return state

    last = count - 1
    sums, flights = [], []
    for i in range(count):
        tokens[i], grad_a, turned, low_term, sums = hold(tokens[i], grad_a, turned, low_term, sums)
        flights = [scatter_send(state, 1, 4) for state in sums]
        made = weight_pass(table, tokens[i], w_base, owners)
        if i < last:
            sums.append(hops(made, 0, 1, 4))
    made, flights = hold(made, flights)
    state = hops(made, 0, 1, 2)
    grad_b = factor_gradient(turned, tokens, adapter_matrix, columns_step, 0, early)
    state, grad_b = hold(state, grad_b)
    if steps > early:
        grad_b = factor_gradient(
            turned, tokens, adapter_matrix, columns_step, early, steps - early, grad_b
        )
    sums = [hops(scatter_take(flight, 1), 2, len(wide_bits), 4) for flight in flights]
    sums.append(hops(state, 1, len(wide_bits), 2))
    results = []
    for (start, rows), parts in zip(pieces, sums):
        summed = jnp.concatenate([part[0] for part in parts], axis=1)
        results.append((summed + low_term[start : start + rows]).astype(jnp.bfloat16))
    return (jnp.concatenate(results, axis=0), grad_a, grad_b)


def solution(mesh):
    return jax.shard_map(
        shards,
        mesh=mesh,
        in_specs=(
            P("wide", "narrow"),
            P("narrow", "wide"),
            P("narrow", "wide"),
            P("narrow", None),
            P(None, "wide"),
        ),
        out_specs=(P("wide", "narrow"), P("narrow", None), P(None, "wide")),
        check_vma=False,
    )
```

```python
import functools

import jax
import jax.numpy as jnp
from jax import lax
from jax.experimental import pallas as pl
from jax.experimental.pallas import tpu as pltpu
from jax.sharding import PartitionSpec as P

adapter_scale = 2.0
piece_rows = 32
weight_rows = 512
vmem_bytes = 40 * 2**20
light = pl.CostEstimate(flops=0, bytes_accessed=2**16, transcendentals=0)


def contract_trailing_axis(left, right):
    return lax.dot_general(
        left, right, (((1,), (1,)), ((), ())), preferred_element_type=jnp.float32
    )


def contract_first(left, right):
    return lax.dot_general(
        left, right, (((0,), (0,)), ((), ())), preferred_element_type=jnp.float32
    )


def bits_of(axis):
    size = lax.axis_size(axis)
    return [1 << i for i in range(size.bit_length() - 1)]


def swap(value, axis, bit):
    size = lax.axis_size(axis)
    return lax.ppermute(value, axis, [(i, i ^ bit) for i in range(size)])


def scatter_small(value, axis):
    me = lax.axis_index(axis)
    for bit in reversed(bits_of(axis)):
        pair = value.reshape(2, value.shape[0] // 2, value.shape[1])
        mine = ((me & bit) != 0).astype(jnp.int32)
        kept = lax.dynamic_index_in_dim(pair, mine, 0, keepdims=False)
        sent = lax.dynamic_index_in_dim(pair, 1 - mine, 0, keepdims=False)
        value = kept + swap(sent, axis, bit)
    return value


def gather_ordered(value, axis, order):
    me = lax.axis_index(axis)
    for bit in order:
        other = swap(value, axis, bit)
        upper = (me & bit) != 0
        value = jnp.concatenate(
            [jnp.where(upper, other, value), jnp.where(upper, value, other)], axis=0
        )
    return value


def phase_a(block, axis):
    return swap(block, axis, 1), swap(block, axis, 2)


def phase_b(block, far, axis):
    return (
        lax.ppermute(block, axis, [(1, 2), (2, 1)]),
        lax.ppermute(far, axis, [(1, 0), (2, 3)]),
    )


def pass_kernel(table, *refs, sources, owners, rows):
    source_refs, refs = refs[:sources], refs[sources:]
    weight, refs = refs[0], refs[1:]
    if sources > 1:
        tokens, kept, sent = refs

        @pl.when(pl.program_id(0) == 0)
        def _():
            size = source_refs[0].shape[0]
            for i, source in enumerate(source_refs[: sources - 2]):
                tokens[i * size : (i + 1) * size] = source[...]
            for end in range(2):

                @pl.when(table[owners] == end)
                def _():
                    tokens[(sources - 2) * size :] = source_refs[sources - 2 + end][...]
    else:
        (tokens,) = source_refs
        kept, sent = refs
    product = contract_trailing_axis(tokens[...], weight[...])
    for i in range(owners):
        place = table[i]
        part = product[i * rows : (i + 1) * rows]

        @pl.when((place & 1) == 0)
        def _():
            kept[place >> 1] = part

        @pl.when((place & 1) == 1)
        def _():
            sent[place >> 1] = part.astype(jnp.bfloat16)


def weight_pass(table, sources, weight, owners):
    depth = weight.shape[1]
    width = weight.shape[0]
    total = sources[0].shape[0] * max(1, len(sources) - 1)
    rows = total // owners
    step = min(weight_rows, width)
    whole = lambda i, *_: (0, 0)
    once = pl.Buffered(1)
    in_specs = [pl.BlockSpec(s.shape, whole, pipeline_mode=once) for s in sources]
    in_specs.append(pl.BlockSpec((step, depth), lambda i, *_: (i, 0)))
    half = (owners // 2, rows, width)
    out_shape = [
        jax.ShapeDtypeStruct(half, jnp.float32),
        jax.ShapeDtypeStruct(half, jnp.bfloat16),
    ]
    out_specs = [pl.BlockSpec((owners // 2, rows, step), lambda i, *_: (0, 0, i))] * 2
    if len(sources) > 1:
        out_shape.insert(0, jax.ShapeDtypeStruct((total, depth), jnp.bfloat16))
        out_specs.insert(0, pl.BlockSpec((total, depth), whole, pipeline_mode=once))
    outs = pl.pallas_call(
        functools.partial(pass_kernel, sources=len(sources), owners=owners, rows=rows),
        grid_spec=pltpu.PrefetchScalarGridSpec(
            num_scalar_prefetch=1,
            grid=(width // step,),
            in_specs=in_specs,
            out_specs=out_specs,
        ),
        out_shape=out_shape,
        compiler_params=pltpu.CompilerParams(vmem_limit_bytes=vmem_bytes),
        cost_estimate=light,
        name="weight_pass",
    )(table, *sources, weight)
    return outs if len(sources) > 1 else [sources[0], *outs]


def factor_kernel(*refs, count, scale):
    acts, tokens, out = refs[:count], refs[count : 2 * count], refs[-1]
    out[...] = scale * sum(
        jnp.dot(a[...], t[...], preferred_element_type=jnp.float32) for a, t in zip(acts, tokens)
    )


def factor_gradient(acts, tokens, scale, step, first, blocks, into=None):
    rank, depth = acts[0].shape[0], tokens[0].shape[1]
    in_specs = [
        pl.BlockSpec(a.shape, lambda i: (0, 0), pipeline_mode=pl.Buffered(1)) for a in acts
    ]
    in_specs += [pl.BlockSpec((t.shape[0], step), lambda i: (0, first + i)) for t in tokens]
    operands = [*acts, *tokens]
    aliases = {}
    if into is not None:
        aliases = {len(operands): 0}
        operands.append(into)
        in_specs.append(pl.BlockSpec(memory_space=pl.ANY))
    return pl.pallas_call(
        functools.partial(factor_kernel, count=len(acts), scale=scale),
        grid=(blocks,),
        in_specs=in_specs,
        out_specs=pl.BlockSpec((rank, step), lambda i: (0, first + i)),
        out_shape=jax.ShapeDtypeStruct((rank, depth), jnp.float32),
        input_output_aliases=aliases,
        compiler_params=pltpu.CompilerParams(vmem_limit_bytes=vmem_bytes),
        cost_estimate=light,
        name="factor_gradient",
    )(*operands)


def scatter_send(state, hop):
    if hop == 0:
        kept, sent = state
        half = kept.shape[2] // 2
        got = [swap(sent[:, :, side * half : (side + 1) * half], "wide", 1) for side in range(2)]
        return kept, got
    bits = bits_of("wide")[:-1]
    stay, got = [], []
    for part, order in zip(state, (bits, bits[::-1])):
        bit = order[hop - 1]
        stay.append({p: part[p] for p in part if not p & bit})
        away = jnp.stack([part[p | bit].astype(jnp.bfloat16) for p in stay[-1]])
        got.append(swap(away, "wide", 2 * bit))
    return stay, got


def scatter_take(flight, hop):
    stay, got = flight
    if hop == 0:
        half = stay.shape[2] // 2
        return [
            {p: stay[p, :, side * half : (side + 1) * half] + got[side][p] for p in range(stay.shape[0])}
            for side in range(2)
        ]
    return [{p: part[p] + new[i] for i, p in enumerate(part)} for part, new in zip(stay, got)]


def hold(*groups):
    leaves, tree = jax.tree.flatten(groups)
    return jax.tree.unflatten(tree, lax.optimization_barrier(leaves))


def cut_rows(owner_rows):
    sizes = [piece_rows] * (owner_rows // piece_rows)
    if not sizes:
        sizes = [owner_rows]
    sizes[0] += owner_rows - sum(sizes)
    starts = [sum(sizes[:i]) for i in range(len(sizes))]
    return list(zip(starts, sizes))


def shards(inputs, grad_out, w_base, adapter_down_matrix, b_factor):
    owner_rows = inputs.shape[0]
    owners = lax.axis_size("wide")
    groups = lax.axis_size("narrow")
    me_wide = lax.axis_index("wide")
    me_narrow = lax.axis_index("narrow")
    adapter_matrix = adapter_scale / (owner_rows * owners)
    share = grad_out.shape[0] // owner_rows
    rank = b_factor.shape[0]
    depth = grad_out.shape[1]
    wide_bits, narrow_bits = bits_of("wide"), bits_of("narrow")
    pieces = cut_rows(owner_rows)
    count = len(pieces)
    line = groups == 4

    held = [me_narrow ^ i if line else jnp.int32(i) for i in range(groups)]
    table = [(block * share + h) ^ me_wide for block in held for h in range(share)]
    table.append(((me_narrow == 0) | (me_narrow == groups - 1)).astype(jnp.int32))
    table = jnp.stack([entry.astype(jnp.int32) for entry in table])

    def block_of(source, i):
        start, rows = pieces[i]
        own = source.reshape(share, owner_rows, depth)
        return own[:, start : start + rows].reshape(share * rows, depth)

    blocks, near, far, middle, onward = {}, {}, {}, {}, {}

    def begin(i):
        if line:
            near[i], far[i] = phase_a(blocks[i], "narrow")
        else:
            near[i] = far[i] = lax.all_gather(blocks[i], "narrow", axis=0, tiled=True)

    def complete(i):
        if line:
            middle[i], onward[i] = phase_b(blocks[i], far[i], "narrow")
        else:
            middle[i], onward[i] = near[i], far[i]

    blocks[0] = block_of(grad_out, 0)
    begin(0)

    blocks[0], low_source = hold(blocks[0], grad_out)
    low_part = contract_trailing_axis(low_source, b_factor)
    low_small = scatter_small(low_part, "wide").astype(jnp.bfloat16)

    low_rows = low_small
    near[0], far[0], blocks[0], grad_out, low_rows, inputs = hold(
        near[0], far[0], blocks[0], grad_out, low_rows, inputs
    )
    complete(0)
    blocks[1] = block_of(grad_out, 1)
    act_part = jnp.dot(inputs, adapter_down_matrix, preferred_element_type=jnp.float32)
    both = jnp.concatenate([act_part.astype(jnp.bfloat16), low_rows], axis=0)
    small = {"inputs": inputs, "both": both}
    small["got"] = [swap(both, "narrow", p) for p in range(1, groups)]

    def take():
        if "both" in small:
            value = jnp.stack([small.pop("both"), *small.pop("got")])
            for bit in narrow_bits:
                cut = value.reshape(groups // (2 * bit), 2, bit, *value.shape[1:])
                value = jnp.where((me_narrow & bit) != 0, cut[:, ::-1], cut).reshape(value.shape)
            act = jnp.sum(value[:, :owner_rows].astype(jnp.float32), axis=0).astype(jnp.bfloat16)
            low = value[:, owner_rows:].reshape(-1, rank)
            small["rows"] = jnp.concatenate([act, low], axis=0)[None]
        elif "got" in small:
            upper = (me_wide & taken.pop(0)) != 0
            name = "rows" if "rows" in small else "grad_a"
            mine, other = small[name], small.pop("got")
            first, second = jnp.where(upper, other, mine), jnp.where(upper, mine, other)
            small[name] = jnp.concatenate([first, second], axis=0)

    taken = wide_bits + wide_bits[::-1]
    bits_left = list(taken)

    def small_hop():
        take()
        if not bits_left:
            return
        if len(bits_left) == len(wide_bits):
            share_made()
        small["got"] = swap(small["rows" if "rows" in small else "grad_a"], "wide", bits_left.pop(0))

    def regroup():
        shares = small.pop("inputs").reshape(owner_rows, owners, -1)
        flipped = [
            sum(bit for i, bit in enumerate(wide_bits) if w & wide_bits[len(wide_bits) - 1 - i])
            for w in range(owners)
        ]
        shares = jnp.stack([shares[:, f] for f in flipped], axis=0)
        columns = lax.all_to_all(shares, "wide", split_axis=0, concat_axis=0)
        small["columns"] = columns.reshape(owner_rows * owners, -1)

    def share_made():
        rows = small.pop("rows")
        low_wide = rows[:, owner_rows:].reshape(owners, groups, low_small.shape[0], rank)
        low_all = jnp.swapaxes(low_wide, 0, 1).reshape(owner_rows * owners, rank)
        low_own = lax.dynamic_slice_in_dim(low_all, me_wide * owner_rows, owner_rows)
        small["term"] = adapter_scale * contract_trailing_axis(low_own, adapter_down_matrix)
        made = adapter_matrix * contract_first(small.pop("columns"), low_all)
        small["grad_a"] = made.astype(jnp.bfloat16)
        acts = rows[:, :owner_rows].reshape(groups, share, owner_rows, rank)
        if line:
            for bit in narrow_bits:
                cut = acts.reshape(groups // (2 * bit), 2, bit, share, owner_rows, rank)
                acts = jnp.where((me_narrow & bit) != 0, cut[:, ::-1], cut).reshape(acts.shape)
        small["turned"] = [
            acts[:, :, start : start + rows].reshape(owners * rows, rank).T
            for start, rows in pieces
        ]

    tokens, sums = {}, {}
    done_hops = {}

    def sum_hop(i):
        if done_hops[i]:
            sums[i] = scatter_take(sums[i], done_hops[i] - 1)
        if done_hops[i] < len(wide_bits):
            sums[i] = scatter_send(sums[i], done_hops[i])
        done_hops[i] += 1

    def step():
        small_hop()
        for i in sums:
            if done_hops[i] <= len(wide_bits):
                sum_hop(i)

    def run_pass(i):
        sources = [blocks[i], near[i], far[i], middle[i], onward[i]] if line else [near[i]]
        tokens[i], kept, sent = weight_pass(table, sources, w_base, owners)
        sums[i] = (kept, sent)
        done_hops[i] = 0

    regroup()
    for i in range(count):
        if i:
            near[i], far[i], blocks, grad_out, small, sums = hold(
                near[i], far[i], blocks, grad_out, small, sums
            )
            complete(i)
            if i + 1 < count:
                blocks[i + 1] = block_of(grad_out, i + 1)
            step()
        middle[i], onward[i], blocks, grad_out, small, sums = hold(
            middle[i], onward[i], blocks, grad_out, small, sums
        )
        if i + 1 < count:
            begin(i + 1)
            step()
            run_pass(i)
    step()
    run_pass(count - 1)
    small, sums = hold(small, sums)
    while bits_left or "got" in small:
        small_hop()
    columns_step = max(128 * c for c in range(1, 14) if depth % (128 * c) == 0)
    steps = depth // columns_step
    early = steps // 2 or 1
    turned = small["turned"]
    tokens = [tokens[i] for i in range(count)]
    sum_hop(count - 1)
    grad_b = factor_gradient(turned, tokens, adapter_matrix, columns_step, 0, early)
    sum_hop(count - 1)
    sums[count - 1], grad_b = hold(sums[count - 1], grad_b)
    if steps > early:
        grad_b = factor_gradient(
            turned, tokens, adapter_matrix, columns_step, early, steps - early, grad_b
        )
    results = []
    for i, (start, rows) in enumerate(pieces):
        while done_hops[i] <= len(wide_bits):
            sum_hop(i)
        mine = small["term"][start : start + rows]
        summed = jnp.concatenate([part[0] for part in sums[i]], axis=1)
        results.append((summed + mine).astype(jnp.bfloat16))
    grad_a = small["grad_a"].astype(jnp.float32)
    return (jnp.concatenate(results, axis=0), grad_a, grad_b)


def solution(mesh):
    return jax.shard_map(
        shards,
        mesh=mesh,
        in_specs=(
            P("wide", "narrow"),
            P("narrow", "wide"),
            P("narrow", "wide"),
            P("narrow", None),
            P(None, "wide"),
        ),
        out_specs=(P("wide", "narrow"), P("narrow", None), P(None, "wide")),
        check_vma=False,
    )
```

```python
import functools

import jax
import jax.numpy as jnp
from jax import lax
from jax.experimental import pallas as pl
from jax.experimental.pallas import tpu as pltpu
from jax.sharding import PartitionSpec as P

adapter_scale = 2.0
piece_rows = 32
weight_rows = 512
vmem_bytes = 40 * 2**20
light = pl.CostEstimate(flops=0, bytes_accessed=2**16, transcendentals=0)


def contract_trailing_axis(left, right):
    return lax.dot_general(
        left, right, (((1,), (1,)), ((), ())), preferred_element_type=jnp.float32
    )


def contract_first(left, right):
    return lax.dot_general(
        left, right, (((0,), (0,)), ((), ())), preferred_element_type=jnp.float32
    )


def bits_of(axis):
    size = lax.axis_size(axis)
    return [1 << i for i in range(size.bit_length() - 1)]


def swap(value, axis, bit):
    size = lax.axis_size(axis)
    return lax.ppermute(value, axis, [(i, i ^ bit) for i in range(size)])


def scatter_small(value, axis):
    me = lax.axis_index(axis)
    for bit in reversed(bits_of(axis)):
        pair = value.reshape(2, value.shape[0] // 2, value.shape[1])
        mine = ((me & bit) != 0).astype(jnp.int32)
        kept = lax.dynamic_index_in_dim(pair, mine, 0, keepdims=False)
        sent = lax.dynamic_index_in_dim(pair, 1 - mine, 0, keepdims=False)
        value = kept + swap(sent, axis, bit)
    return value


def gather_ordered(value, axis, order):
    me = lax.axis_index(axis)
    for bit in order:
        other = swap(value, axis, bit)
        upper = (me & bit) != 0
        value = jnp.concatenate(
            [jnp.where(upper, other, value), jnp.where(upper, value, other)], axis=0
        )
    return value


def phase_a(block, axis):
    return swap(block, axis, 1), swap(block, axis, 2)


def phase_b(block, far, axis):
    return (
        lax.ppermute(block, axis, [(1, 2), (2, 1)]),
        lax.ppermute(far, axis, [(1, 0), (2, 3)]),
    )


def pass_kernel(table, *refs, sources, owners, rows):
    source_refs, refs = refs[:sources], refs[sources:]
    weight, refs = refs[0], refs[1:]
    if sources > 1:
        tokens, kept, sent = refs

        @pl.when(pl.program_id(0) == 0)
        def _():
            size = source_refs[0].shape[0]
            for i, source in enumerate(source_refs[: sources - 2]):
                tokens[i * size : (i + 1) * size] = source[...]
            for end in range(2):

                @pl.when(table[owners] == end)
                def _():
                    tokens[(sources - 2) * size :] = source_refs[sources - 2 + end][...]
    else:
        (tokens,) = source_refs
        kept, sent = refs
    product = contract_trailing_axis(tokens[...], weight[...])
    for i in range(owners):
        place = table[i]
        part = product[i * rows : (i + 1) * rows]

        @pl.when((place & 1) == 0)
        def _():
            kept[place >> 1] = part

        @pl.when((place & 1) == 1)
        def _():
            sent[place >> 1] = part.astype(jnp.bfloat16)


def weight_pass(table, sources, weight, owners):
    depth = weight.shape[1]
    width = weight.shape[0]
    total = sources[0].shape[0] * max(1, len(sources) - 1)
    rows = total // owners
    step = min(weight_rows, width)
    whole = lambda i, *_: (0, 0)
    once = pl.Buffered(1)
    in_specs = [pl.BlockSpec(s.shape, whole, pipeline_mode=once) for s in sources]
    in_specs.append(pl.BlockSpec((step, depth), lambda i, *_: (i, 0)))
    half = (owners // 2, rows, width)
    out_shape = [
        jax.ShapeDtypeStruct(half, jnp.float32),
        jax.ShapeDtypeStruct(half, jnp.bfloat16),
    ]
    out_specs = [pl.BlockSpec((owners // 2, rows, step), lambda i, *_: (0, 0, i))] * 2
    if len(sources) > 1:
        out_shape.insert(0, jax.ShapeDtypeStruct((total, depth), jnp.bfloat16))
        out_specs.insert(0, pl.BlockSpec((total, depth), whole, pipeline_mode=once))
    outs = pl.pallas_call(
        functools.partial(pass_kernel, sources=len(sources), owners=owners, rows=rows),
        grid_spec=pltpu.PrefetchScalarGridSpec(
            num_scalar_prefetch=1,
            grid=(width // step,),
            in_specs=in_specs,
            out_specs=out_specs,
        ),
        out_shape=out_shape,
        compiler_params=pltpu.CompilerParams(vmem_limit_bytes=vmem_bytes),
        cost_estimate=light,
        name="weight_pass",
    )(table, *sources, weight)
    return outs if len(sources) > 1 else [sources[0], *outs]


def factor_kernel(order, acts, *refs, pieces, scale):
    tokens, out, lined = refs[: len(pieces)], refs[-2], refs[-1]
    owners = acts.shape[0]

    @pl.when(pl.program_id(0) == 0)
    def _():
        base = 0
        for start, rows in pieces:
            for i in range(owners):
                lined[base : base + rows] = acts[order[i], start : start + rows, :]
                base += rows

    base, total = 0, None
    for token in tokens:
        size = token.shape[0]
        part = contract_first(lined[base : base + size], token[...])
        total = part if total is None else total + part
        base += size
    out[...] = scale * total


def factor_gradient(order, acts, tokens, pieces, scale, step, first, blocks, into=None):
    rank, depth = acts.shape[2], tokens[0].shape[1]
    in_specs = [
        pl.BlockSpec(acts.shape, lambda i, *_: (0, 0, 0), pipeline_mode=pl.Buffered(1))
    ]
    in_specs += [pl.BlockSpec((t.shape[0], step), lambda i, *_: (0, first + i)) for t in tokens]
    operands = [acts, *tokens]
    aliases = {}
    if into is not None:
        aliases = {1 + len(operands): 0}
        operands.append(into)
        in_specs.append(pl.BlockSpec(memory_space=pl.ANY))
    return pl.pallas_call(
        functools.partial(factor_kernel, pieces=pieces, scale=scale),
        grid_spec=pltpu.PrefetchScalarGridSpec(
            num_scalar_prefetch=1,
            grid=(blocks,),
            in_specs=in_specs,
            out_specs=pl.BlockSpec((rank, step), lambda i, *_: (0, first + i)),
            scratch_shapes=[pltpu.VMEM((sum(t.shape[0] for t in tokens), rank), jnp.bfloat16)],
        ),
        out_shape=jax.ShapeDtypeStruct((rank, depth), jnp.float32),
        input_output_aliases=aliases,
        compiler_params=pltpu.CompilerParams(vmem_limit_bytes=vmem_bytes),
        cost_estimate=light,
        name="factor_gradient",
    )(order, *operands)


def scatter_send(state, hop):
    if hop == 0:
        kept, sent = state
        half = kept.shape[2] // 2
        got = [swap(sent[:, :, side * half : (side + 1) * half], "wide", 1) for side in range(2)]
        return kept, got
    bits = bits_of("wide")[:-1]
    stay, got = [], []
    for part, order in zip(state, (bits, bits[::-1])):
        bit = order[hop - 1]
        stay.append({p: part[p] for p in part if not p & bit})
        away = jnp.stack([part[p | bit].astype(jnp.bfloat16) for p in stay[-1]])
        got.append(swap(away, "wide", 2 * bit))
    return stay, got


def scatter_take(flight, hop):
    stay, got = flight
    if hop == 0:
        half = stay.shape[2] // 2
        return [
            {p: stay[p, :, side * half : (side + 1) * half] + got[side][p] for p in range(stay.shape[0])}
            for side in range(2)
        ]
    return [{p: part[p] + new[i] for i, p in enumerate(part)} for part, new in zip(stay, got)]


def hold(*groups):
    leaves, tree = jax.tree.flatten(groups)
    return jax.tree.unflatten(tree, lax.optimization_barrier(leaves))


def cut_rows(owner_rows):
    sizes = [piece_rows] * (owner_rows // piece_rows)
    if not sizes:
        sizes = [owner_rows]
    sizes[0] += owner_rows - sum(sizes)
    starts = [sum(sizes[:i]) for i in range(len(sizes))]
    return list(zip(starts, sizes))


def shards(inputs, grad_out, w_base, adapter_down_matrix, b_factor):
    owner_rows = inputs.shape[0]
    owners = lax.axis_size("wide")
    groups = lax.axis_size("narrow")
    me_wide = lax.axis_index("wide")
    me_narrow = lax.axis_index("narrow")
    adapter_matrix = adapter_scale / (owner_rows * owners)
    share = grad_out.shape[0] // owner_rows
    rank = b_factor.shape[0]
    depth = grad_out.shape[1]
    wide_bits, narrow_bits = bits_of("wide"), bits_of("narrow")
    pieces = cut_rows(owner_rows)
    count = len(pieces)
    line = groups == 4

    held = [me_narrow ^ i if line else jnp.int32(i) for i in range(groups)]
    table = [(block * share + h) ^ me_wide for block in held for h in range(share)]
    order = jnp.stack([block * share + h for block in held for h in range(share)]).astype(jnp.int32)
    table.append(((me_narrow == 0) | (me_narrow == groups - 1)).astype(jnp.int32))
    table = jnp.stack([entry.astype(jnp.int32) for entry in table])

    def block_of(source, i):
        start, rows = pieces[i]
        own = source.reshape(share, owner_rows, depth)
        return own[:, start : start + rows].reshape(share * rows, depth)

    blocks, near, far, middle, onward = {}, {}, {}, {}, {}

    def begin(i):
        if line:
            near[i], far[i] = phase_a(blocks[i], "narrow")
        else:
            near[i] = far[i] = lax.all_gather(blocks[i], "narrow", axis=0, tiled=True)

    def complete(i):
        if line:
            middle[i], onward[i] = phase_b(blocks[i], far[i], "narrow")
        else:
            middle[i], onward[i] = near[i], far[i]

    blocks[0] = block_of(grad_out, 0)
    begin(0)

    blocks[0], low_source = hold(blocks[0], grad_out)
    low_part = contract_trailing_axis(low_source, b_factor)
    low_small = scatter_small(low_part, "wide").astype(jnp.bfloat16)

    low_rows = low_small
    near[0], far[0], blocks[0], grad_out, low_rows, inputs = hold(
        near[0], far[0], blocks[0], grad_out, low_rows, inputs
    )
    complete(0)
    blocks[1] = block_of(grad_out, 1)
    act_part = jnp.dot(inputs, adapter_down_matrix, preferred_element_type=jnp.float32)
    both = jnp.concatenate([act_part.astype(jnp.bfloat16), low_rows], axis=0)
    small = {"inputs": inputs, "both": both}
    small["got"] = [swap(both, "narrow", p) for p in range(1, groups)]

    def take():
        if "both" in small:
            value = jnp.stack([small.pop("both"), *small.pop("got")])
            for bit in narrow_bits:
                cut = value.reshape(groups // (2 * bit), 2, bit, *value.shape[1:])
                value = jnp.where((me_narrow & bit) != 0, cut[:, ::-1], cut).reshape(value.shape)
            act = jnp.sum(value[:, :owner_rows].astype(jnp.float32), axis=0).astype(jnp.bfloat16)
            low = value[:, owner_rows:].reshape(-1, rank)
            small["rows"] = jnp.concatenate([act, low], axis=0)[None]
        elif "got" in small:
            upper = (me_wide & taken.pop(0)) != 0
            name = "rows" if "rows" in small else "grad_a"
            mine, other = small[name], small.pop("got")
            first, second = jnp.where(upper, other, mine), jnp.where(upper, mine, other)
            small[name] = jnp.concatenate([first, second], axis=0)

    taken = wide_bits + wide_bits[::-1]
    bits_left = list(taken)

    def small_hop():
        take()
        if not bits_left:
            return
        if len(bits_left) == len(wide_bits):
            share_made()
        small["got"] = swap(small["rows" if "rows" in small else "grad_a"], "wide", bits_left.pop(0))

    def regroup():
        shares = small.pop("inputs").reshape(owner_rows, owners, -1)
        flipped = [
            sum(bit for i, bit in enumerate(wide_bits) if w & wide_bits[len(wide_bits) - 1 - i])
            for w in range(owners)
        ]
        shares = jnp.stack([shares[:, f] for f in flipped], axis=0)
        columns = lax.all_to_all(shares, "wide", split_axis=0, concat_axis=0)
        small["columns"] = columns.reshape(owner_rows * owners, -1)

    def share_made():
        rows = small.pop("rows")
        low_wide = rows[:, owner_rows:].reshape(owners, groups, low_small.shape[0], rank)
        low_all = jnp.swapaxes(low_wide, 0, 1).reshape(owner_rows * owners, rank)
        low_own = lax.dynamic_slice_in_dim(low_all, me_wide * owner_rows, owner_rows)
        small["term"] = adapter_scale * contract_trailing_axis(low_own, adapter_down_matrix)
        made = adapter_matrix * contract_first(small.pop("columns"), low_all)
        small["grad_a"] = made.astype(jnp.bfloat16)
        small["acts"] = rows[:, :owner_rows]

    tokens, sums = {}, {}
    done_hops = {}

    def sum_hop(i):
        if done_hops[i]:
            sums[i] = scatter_take(sums[i], done_hops[i] - 1)
        if done_hops[i] < len(wide_bits):
            sums[i] = scatter_send(sums[i], done_hops[i])
        done_hops[i] += 1

    def step(small_hops=1):
        for _ in range(small_hops):
            small_hop()
        for i in sums:
            if done_hops[i] <= len(wide_bits):
                sum_hop(i)

    def run_pass(i):
        sources = [blocks[i], near[i], far[i], middle[i], onward[i]] if line else [near[i]]
        tokens[i], kept, sent = weight_pass(table, sources, w_base, owners)
        sums[i] = (kept, sent)
        done_hops[i] = 0
        if i + 2 == count:
            sums.update(hold(sums)[0])
            sum_hop(i)

    regroup()
    for i in range(count):
        if i:
            near[i], far[i], blocks, grad_out, small, sums = hold(
                near[i], far[i], blocks, grad_out, small, sums
            )
            complete(i)
            if i + 1 < count:
                blocks[i + 1] = block_of(grad_out, i + 1)
            step(2 if i == 1 else 1)
        middle[i], onward[i], blocks, grad_out, small, sums = hold(
            middle[i], onward[i], blocks, grad_out, small, sums
        )
        if i + 1 < count:
            begin(i + 1)
            step(1 if i == 0 else 0)
            run_pass(i)
    step()
    run_pass(count - 1)
    small, sums = hold(small, sums)
    columns_step = max(128 * c for c in range(1, 14) if depth % (128 * c) == 0)
    steps = depth // columns_step
    early = steps // 2 or 1
    tokens = [tokens[i] for i in range(count)]
    last = count - 1

    def factor(first, blocks, into=None):
        return factor_gradient(
            order, small["acts"], tokens, pieces, adapter_matrix, columns_step, first, blocks, into
        )

    sum_hop(last)
    while bits_left or "got" in small:
        small_hop()
    grad_a = small["grad_a"].astype(jnp.float32)
    grad_b = factor(0, early)
    sum_hop(last)
    sums[last], grad_a, grad_b = hold(sums[last], grad_a, grad_b)
    if steps > early:
        grad_b = factor(early, steps - early, grad_b)
    results = []
    for i, (start, rows) in enumerate(pieces):
        while done_hops[i] <= len(wide_bits):
            sum_hop(i)
        mine = small["term"][start : start + rows]
        summed = jnp.concatenate([part[0] for part in sums[i]], axis=1)
        results.append((summed + mine).astype(jnp.bfloat16))
    return (jnp.concatenate(results, axis=0), grad_a, grad_b)


def solution(mesh):
    return jax.shard_map(
        shards,
        mesh=mesh,
        in_specs=(
            P("wide", "narrow"),
            P("narrow", "wide"),
            P("narrow", "wide"),
            P("narrow", None),
            P(None, "wide"),
        ),
        out_specs=(P("wide", "narrow"), P("narrow", None), P(None, "wide")),
        check_vma=False,
    )
```

```python
import functools

import jax
import jax.numpy as jnp
from jax import lax
from jax.experimental import pallas as pl
from jax.experimental.pallas import tpu as pltpu
from jax.sharding import PartitionSpec as P

adapter_scale = 2.0
piece_rows = 32
weight_rows = 512
vmem_bytes = 40 * 2**20
light = pl.CostEstimate(flops=0, bytes_accessed=2**16, transcendentals=0)


def contract_trailing_axis(left, right):
    return lax.dot_general(
        left, right, (((1,), (1,)), ((), ())), preferred_element_type=jnp.float32
    )


def contract_first(left, right):
    return lax.dot_general(
        left, right, (((0,), (0,)), ((), ())), preferred_element_type=jnp.float32
    )


def bits_of(axis):
    size = lax.axis_size(axis)
    return [1 << i for i in range(size.bit_length() - 1)]


def swap(value, axis, bit):
    size = lax.axis_size(axis)
    return lax.ppermute(value, axis, [(i, i ^ bit) for i in range(size)])


def scatter_small(value, axis):
    me = lax.axis_index(axis)
    for bit in reversed(bits_of(axis)):
        pair = value.reshape(2, value.shape[0] // 2, value.shape[1])
        mine = ((me & bit) != 0).astype(jnp.int32)
        kept = lax.dynamic_index_in_dim(pair, mine, 0, keepdims=False)
        sent = lax.dynamic_index_in_dim(pair, 1 - mine, 0, keepdims=False)
        value = kept + swap(sent, axis, bit)
    return value


def gather_ordered(value, axis, order):
    me = lax.axis_index(axis)
    for bit in order:
        other = swap(value, axis, bit)
        upper = (me & bit) != 0
        value = jnp.concatenate(
            [jnp.where(upper, other, value), jnp.where(upper, value, other)], axis=0
        )
    return value


def phase_a(block, axis):
    return swap(block, axis, 1), swap(block, axis, 2)


def phase_b(block, far, axis):
    return (
        lax.ppermute(block, axis, [(1, 2), (2, 1)]),
        lax.ppermute(far, axis, [(1, 0), (2, 3)]),
    )


def pass_kernel(table, *refs, sources, owners, rows):
    source_refs, refs = refs[:sources], refs[sources:]
    weight, refs = refs[0], refs[1:]
    if sources > 1:
        tokens, kept, sent = refs

        @pl.when(pl.program_id(0) == 0)
        def _():
            size = source_refs[0].shape[0]
            for i, source in enumerate(source_refs[: sources - 2]):
                tokens[i * size : (i + 1) * size] = source[...]
            for end in range(2):

                @pl.when(table[owners] == end)
                def _():
                    tokens[(sources - 2) * size :] = source_refs[sources - 2 + end][...]
    else:
        (tokens,) = source_refs
        kept, sent = refs
    product = contract_trailing_axis(tokens[...], weight[...])
    for i in range(owners):
        place = table[i]
        part = product[i * rows : (i + 1) * rows]

        @pl.when((place & 1) == 0)
        def _():
            kept[place >> 1] = part

        @pl.when((place & 1) == 1)
        def _():
            sent[place >> 1] = part.astype(jnp.bfloat16)


def weight_pass(table, sources, weight, owners):
    depth = weight.shape[1]
    width = weight.shape[0]
    total = sources[0].shape[0] * max(1, len(sources) - 1)
    rows = total // owners
    step = min(weight_rows, width)
    whole = lambda i, *_: (0, 0)
    once = pl.Buffered(1)
    in_specs = [pl.BlockSpec(s.shape, whole, pipeline_mode=once) for s in sources]
    in_specs.append(pl.BlockSpec((step, depth), lambda i, *_: (i, 0)))
    half = (owners // 2, rows, width)
    out_shape = [
        jax.ShapeDtypeStruct(half, jnp.float32),
        jax.ShapeDtypeStruct(half, jnp.bfloat16),
    ]
    out_specs = [pl.BlockSpec((owners // 2, rows, step), lambda i, *_: (0, 0, i))] * 2
    if len(sources) > 1:
        out_shape.insert(0, jax.ShapeDtypeStruct((total, depth), jnp.bfloat16))
        out_specs.insert(0, pl.BlockSpec((total, depth), whole, pipeline_mode=once))
    outs = pl.pallas_call(
        functools.partial(pass_kernel, sources=len(sources), owners=owners, rows=rows),
        grid_spec=pltpu.PrefetchScalarGridSpec(
            num_scalar_prefetch=1,
            grid=(width // step,),
            in_specs=in_specs,
            out_specs=out_specs,
        ),
        out_shape=out_shape,
        compiler_params=pltpu.CompilerParams(vmem_limit_bytes=vmem_bytes),
        cost_estimate=light,
        name="weight_pass",
    )(table, *sources, weight)
    return outs if len(sources) > 1 else [sources[0], *outs]


def factor_kernel(order, acts, *refs, pieces, scale):
    tokens, out, lined = refs[: len(pieces)], refs[-2], refs[-1]
    owners = acts.shape[0]

    @pl.when(pl.program_id(0) == 0)
    def _():
        base = 0
        for start, rows in pieces:
            for i in range(owners):
                lined[base : base + rows] = acts[order[i], start : start + rows, :]
                base += rows

    base, total = 0, None
    for token in tokens:
        size = token.shape[0]
        part = contract_first(lined[base : base + size], token[...])
        total = part if total is None else total + part
        base += size
    out[...] = scale * total


def factor_gradient(order, acts, tokens, pieces, scale, step, first, blocks, into=None):
    rank, depth = acts.shape[2], tokens[0].shape[1]
    in_specs = [
        pl.BlockSpec(acts.shape, lambda i, *_: (0, 0, 0), pipeline_mode=pl.Buffered(1))
    ]
    in_specs += [pl.BlockSpec((t.shape[0], step), lambda i, *_: (0, first + i)) for t in tokens]
    operands = [acts, *tokens]
    aliases = {}
    if into is not None:
        aliases = {1 + len(operands): 0}
        operands.append(into)
        in_specs.append(pl.BlockSpec(memory_space=pl.ANY))
    return pl.pallas_call(
        functools.partial(factor_kernel, pieces=pieces, scale=scale),
        grid_spec=pltpu.PrefetchScalarGridSpec(
            num_scalar_prefetch=1,
            grid=(blocks,),
            in_specs=in_specs,
            out_specs=pl.BlockSpec((rank, step), lambda i, *_: (0, first + i)),
            scratch_shapes=[pltpu.VMEM((sum(t.shape[0] for t in tokens), rank), jnp.bfloat16)],
        ),
        out_shape=jax.ShapeDtypeStruct((rank, depth), jnp.float32),
        input_output_aliases=aliases,
        compiler_params=pltpu.CompilerParams(vmem_limit_bytes=vmem_bytes),
        cost_estimate=light,
        name="factor_gradient",
    )(order, *operands)


def scatter_send(state, hop):
    if hop == 0:
        kept, sent = state
        half = kept.shape[2] // 2
        got = [swap(sent[:, :, side * half : (side + 1) * half], "wide", 1) for side in range(2)]
        return kept, got
    bits = bits_of("wide")[:-1]
    stay, got = [], []
    for part, order in zip(state, (bits, bits[::-1])):
        bit = order[hop - 1]
        stay.append({p: part[p] for p in part if not p & bit})
        away = jnp.stack([part[p | bit].astype(jnp.bfloat16) for p in stay[-1]])
        got.append(swap(away, "wide", 2 * bit))
    return stay, got


def scatter_take(flight, hop):
    stay, got = flight
    if hop == 0:
        half = stay.shape[2] // 2
        return [
            {p: stay[p, :, side * half : (side + 1) * half] + got[side][p] for p in range(stay.shape[0])}
            for side in range(2)
        ]
    return [{p: part[p] + new[i] for i, p in enumerate(part)} for part, new in zip(stay, got)]


def hold(*groups):
    leaves, tree = jax.tree.flatten(groups)
    return jax.tree.unflatten(tree, lax.optimization_barrier(leaves))


def cut_rows(owner_rows):
    sizes = [piece_rows] * (owner_rows // piece_rows)
    if not sizes:
        sizes = [owner_rows]
    sizes[0] += owner_rows - sum(sizes)
    starts = [sum(sizes[:i]) for i in range(len(sizes))]
    return list(zip(starts, sizes))


def shards(inputs, grad_out, w_base, adapter_down_matrix, b_factor):
    owner_rows = inputs.shape[0]
    owners = lax.axis_size("wide")
    groups = lax.axis_size("narrow")
    me_wide = lax.axis_index("wide")
    me_narrow = lax.axis_index("narrow")
    adapter_matrix = adapter_scale / (owner_rows * owners)
    share = grad_out.shape[0] // owner_rows
    rank = b_factor.shape[0]
    depth = grad_out.shape[1]
    wide_bits, narrow_bits = bits_of("wide"), bits_of("narrow")
    pieces = cut_rows(owner_rows)
    count = len(pieces)
    line = groups == 4

    held = [me_narrow ^ i if line else jnp.int32(i) for i in range(groups)]
    table = [(block * share + h) ^ me_wide for block in held for h in range(share)]
    order = jnp.stack([block * share + h for block in held for h in range(share)]).astype(jnp.int32)
    table.append(((me_narrow == 0) | (me_narrow == groups - 1)).astype(jnp.int32))
    table = jnp.stack([entry.astype(jnp.int32) for entry in table])

    def block_of(source, i):
        start, rows = pieces[i]
        own = source.reshape(share, owner_rows, depth)
        return own[:, start : start + rows].reshape(share * rows, depth)

    blocks, near, far, middle, onward = {}, {}, {}, {}, {}

    def begin(i):
        if line:
            near[i], far[i] = phase_a(blocks[i], "narrow")
        else:
            near[i] = far[i] = lax.all_gather(blocks[i], "narrow", axis=0, tiled=True)

    def complete(i):
        if line:
            middle[i], onward[i] = phase_b(blocks[i], far[i], "narrow")
        else:
            middle[i], onward[i] = near[i], far[i]

    blocks[0] = block_of(grad_out, 0)
    begin(0)

    blocks[0], low_source = hold(blocks[0], grad_out)
    low_part = contract_trailing_axis(low_source, b_factor)
    low_small = scatter_small(low_part, "wide").astype(jnp.bfloat16)

    low_rows = low_small
    near[0], far[0], blocks[0], grad_out, low_rows, inputs = hold(
        near[0], far[0], blocks[0], grad_out, low_rows, inputs
    )
    complete(0)
    blocks[1] = block_of(grad_out, 1)
    act_part = jnp.dot(inputs, adapter_down_matrix, preferred_element_type=jnp.float32)
    both = jnp.concatenate([act_part.astype(jnp.bfloat16), low_rows], axis=0)
    small = {"inputs": inputs, "both": both}
    small["got"] = [swap(both, "narrow", p) for p in range(1, groups)]

    def take():
        if "both" in small:
            value = jnp.stack([small.pop("both"), *small.pop("got")])
            for bit in narrow_bits:
                cut = value.reshape(groups // (2 * bit), 2, bit, *value.shape[1:])
                value = jnp.where((me_narrow & bit) != 0, cut[:, ::-1], cut).reshape(value.shape)
            act = jnp.sum(value[:, :owner_rows].astype(jnp.float32), axis=0).astype(jnp.bfloat16)
            low = value[:, owner_rows:].reshape(-1, rank)
            small["rows"] = jnp.concatenate([act, low], axis=0)[None]
        elif "got" in small:
            upper = (me_wide & taken.pop(0)) != 0
            name = "rows" if "rows" in small else "grad_a"
            mine, other = small[name], small.pop("got")
            first, second = jnp.where(upper, other, mine), jnp.where(upper, mine, other)
            small[name] = jnp.concatenate([first, second], axis=0)

    taken = wide_bits + wide_bits[::-1]
    bits_left = list(taken)

    def small_hop():
        take()
        if not bits_left:
            return
        prepare()
        small["got"] = swap(small["rows" if "rows" in small else "grad_a"], "wide", bits_left.pop(0))

    def prepare():
        if len(bits_left) <= len(wide_bits) and "rows" in small:
            take()
            share_made()

    def regroup():
        shares = small.pop("inputs").reshape(owner_rows, owners, -1)
        flipped = [
            sum(bit for i, bit in enumerate(wide_bits) if w & wide_bits[len(wide_bits) - 1 - i])
            for w in range(owners)
        ]
        shares = jnp.stack([shares[:, f] for f in flipped], axis=0)
        columns = lax.all_to_all(shares, "wide", split_axis=0, concat_axis=0)
        small["columns"] = columns.reshape(owner_rows * owners, -1)

    def share_made():
        rows = small.pop("rows")
        low_wide = rows[:, owner_rows:].reshape(owners, groups, low_small.shape[0], rank)
        low_all = jnp.swapaxes(low_wide, 0, 1).reshape(owner_rows * owners, rank)
        low_own = lax.dynamic_slice_in_dim(low_all, me_wide * owner_rows, owner_rows)
        small["term"] = adapter_scale * contract_trailing_axis(low_own, adapter_down_matrix)
        made = adapter_matrix * contract_first(small.pop("columns"), low_all)
        small["grad_a"] = made.astype(jnp.bfloat16)
        small["acts"] = rows[:, :owner_rows]

    tokens, sums = {}, {}
    done_hops = {}

    def sum_hop(i):
        if done_hops[i]:
            sums[i] = scatter_take(sums[i], done_hops[i] - 1)
        if done_hops[i] < len(wide_bits):
            sums[i] = scatter_send(sums[i], done_hops[i])
        done_hops[i] += 1

    def step(small_hops=1):
        for _ in range(small_hops):
            small_hop()
        for i in sums:
            if done_hops[i] <= len(wide_bits):
                sum_hop(i)

    def run_pass(i):
        sources = [blocks[i], near[i], far[i], middle[i], onward[i]] if line else [near[i]]
        tokens[i], kept, sent = weight_pass(table, sources, w_base, owners)
        sums[i] = (kept, sent)
        done_hops[i] = 0
        if i + 2 == count:
            sums.update(hold(sums)[0])
            sum_hop(i)

    regroup()
    for i in range(count):
        if i:
            near[i], far[i], blocks, grad_out, small, sums = hold(
                near[i], far[i], blocks, grad_out, small, sums
            )
            complete(i)
            if i + 1 < count:
                blocks[i + 1] = block_of(grad_out, i + 1)
            step(2 if i == 1 else 1)
        middle[i], onward[i], blocks, grad_out, small, sums = hold(
            middle[i], onward[i], blocks, grad_out, small, sums
        )
        if i + 1 < count:
            begin(i + 1)
            step(1 if i == 0 else 0)
            prepare()
            run_pass(i)
    step()
    run_pass(count - 1)
    small, sums = hold(small, sums)
    columns_step = max(128 * c for c in range(1, 5) if depth % (128 * c) == 0)
    steps = depth // columns_step
    early = steps // 2 or 1
    tokens = [tokens[i] for i in range(count)]
    last = count - 1

    def factor(first, blocks, into=None):
        return factor_gradient(
            order, small["acts"], tokens, pieces, adapter_matrix, columns_step, first, blocks, into
        )

    sum_hop(last)
    while bits_left or "got" in small:
        small_hop()
    grad_a = small["grad_a"].astype(jnp.float32)
    grad_b = factor(0, early)
    sum_hop(last)
    sums[last], grad_a, grad_b = hold(sums[last], grad_a, grad_b)
    if steps > early:
        grad_b = factor(early, steps - early, grad_b)
    results = []
    for i, (start, rows) in enumerate(pieces):
        while done_hops[i] <= len(wide_bits):
            sum_hop(i)
        mine = small["term"][start : start + rows]
        summed = jnp.concatenate([part[0] for part in sums[i]], axis=1)
        results.append((summed + mine).astype(jnp.bfloat16))
    return (jnp.concatenate(results, axis=0), grad_a, grad_b)


def solution(mesh):
    return jax.shard_map(
        shards,
        mesh=mesh,
        in_specs=(
            P("wide", "narrow"),
            P("narrow", "wide"),
            P("narrow", "wide"),
            P("narrow", None),
            P(None, "wide"),
        ),
        out_specs=(P("wide", "narrow"), P("narrow", None), P(None, "wide")),
        check_vma=False,
    )
```

```python
import functools

import jax
import jax.numpy as jnp
from jax import lax
from jax.experimental import pallas as pl
from jax.experimental.pallas import tpu as pltpu
from jax.sharding import PartitionSpec as P

adapter_scale = 2.0
piece_rows = 32
weight_rows = 512
vmem_bytes = 40 * 2**20
light = pl.CostEstimate(flops=0, bytes_accessed=2**16, transcendentals=0)


def contract_trailing_axis(left, right):
    return lax.dot_general(
        left, right, (((1,), (1,)), ((), ())), preferred_element_type=jnp.float32
    )


def contract_first(left, right):
    return lax.dot_general(
        left, right, (((0,), (0,)), ((), ())), preferred_element_type=jnp.float32
    )


def bits_of(axis):
    size = lax.axis_size(axis)
    return [1 << i for i in range(size.bit_length() - 1)]


def swap(value, axis, bit):
    size = lax.axis_size(axis)
    return lax.ppermute(value, axis, [(i, i ^ bit) for i in range(size)])


def scatter_small(value, axis):
    me = lax.axis_index(axis)
    for bit in reversed(bits_of(axis)):
        pair = value.reshape(2, value.shape[0] // 2, value.shape[1])
        mine = ((me & bit) != 0).astype(jnp.int32)
        kept = lax.dynamic_index_in_dim(pair, mine, 0, keepdims=False)
        sent = lax.dynamic_index_in_dim(pair, 1 - mine, 0, keepdims=False)
        value = kept + swap(sent, axis, bit)
    return value


def gather_ordered(value, axis, order):
    me = lax.axis_index(axis)
    for bit in order:
        other = swap(value, axis, bit)
        upper = (me & bit) != 0
        value = jnp.concatenate(
            [jnp.where(upper, other, value), jnp.where(upper, value, other)], axis=0
        )
    return value


def phase_a(block, axis):
    return swap(block, axis, 1), swap(block, axis, 2)


def phase_b(block, far, axis):
    return (
        lax.ppermute(block, axis, [(1, 2), (2, 1)]),
        lax.ppermute(far, axis, [(1, 0), (2, 3)]),
    )


def pass_kernel(table, *refs, sources, owners, rows):
    source_refs, refs = refs[:sources], refs[sources:]
    weight, refs = refs[0], refs[1:]
    if sources > 1:
        tokens, kept, sent = refs

        @pl.when(pl.program_id(0) == 0)
        def _():
            size = source_refs[0].shape[0]
            for i, source in enumerate(source_refs[: sources - 2]):
                tokens[i * size : (i + 1) * size] = source[...]
            for end in range(2):

                @pl.when(table[owners] == end)
                def _():
                    tokens[(sources - 2) * size :] = source_refs[sources - 2 + end][...]
    else:
        (tokens,) = source_refs
        kept, sent = refs
    product = contract_trailing_axis(tokens[...], weight[...])
    for i in range(owners):
        place = table[i]
        part = product[i * rows : (i + 1) * rows]

        @pl.when((place & 1) == 0)
        def _():
            kept[place >> 1] = part

        @pl.when((place & 1) == 1)
        def _():
            sent[place >> 1] = part.astype(jnp.bfloat16)


def weight_pass(table, sources, weight, owners):
    depth = weight.shape[1]
    width = weight.shape[0]
    total = sources[0].shape[0] * max(1, len(sources) - 1)
    rows = total // owners
    step = min(weight_rows, width)
    whole = lambda i, *_: (0, 0)
    once = pl.Buffered(1)
    in_specs = [pl.BlockSpec(s.shape, whole, pipeline_mode=once) for s in sources]
    in_specs.append(pl.BlockSpec((step, depth), lambda i, *_: (i, 0)))
    half = (owners // 2, rows, width)
    out_shape = [
        jax.ShapeDtypeStruct(half, jnp.float32),
        jax.ShapeDtypeStruct(half, jnp.bfloat16),
    ]
    out_specs = [pl.BlockSpec((owners // 2, rows, step), lambda i, *_: (0, 0, i))] * 2
    if len(sources) > 1:
        out_shape.insert(0, jax.ShapeDtypeStruct((total, depth), jnp.bfloat16))
        out_specs.insert(0, pl.BlockSpec((total, depth), whole, pipeline_mode=once))
    outs = pl.pallas_call(
        functools.partial(pass_kernel, sources=len(sources), owners=owners, rows=rows),
        grid_spec=pltpu.PrefetchScalarGridSpec(
            num_scalar_prefetch=1,
            grid=(width // step,),
            in_specs=in_specs,
            out_specs=out_specs,
        ),
        out_shape=out_shape,
        compiler_params=pltpu.CompilerParams(vmem_limit_bytes=vmem_bytes),
        cost_estimate=light,
        name="weight_pass",
    )(table, *sources, weight)
    return outs if len(sources) > 1 else [sources[0], *outs]


def factor_kernel(order, acts, *refs, pieces, scale):
    tokens, out, lined = refs[: len(pieces)], refs[-2], refs[-1]
    owners = acts.shape[0]

    @pl.when(pl.program_id(0) == 0)
    def _():
        base = 0
        for start, rows in pieces:
            for i in range(owners):
                lined[base : base + rows] = acts[order[i], start : start + rows, :]
                base += rows

    base, total = 0, None
    for token in tokens:
        size = token.shape[0]
        part = contract_first(lined[base : base + size], token[...])
        total = part if total is None else total + part
        base += size
    out[...] = scale * total


def factor_gradient(order, acts, tokens, pieces, scale, step, first, blocks, into=None):
    rank, depth = acts.shape[2], tokens[0].shape[1]
    in_specs = [
        pl.BlockSpec(acts.shape, lambda i, *_: (0, 0, 0), pipeline_mode=pl.Buffered(1))
    ]
    in_specs += [pl.BlockSpec((t.shape[0], step), lambda i, *_: (0, first + i)) for t in tokens]
    operands = [acts, *tokens]
    aliases = {}
    if into is not None:
        aliases = {1 + len(operands): 0}
        operands.append(into)
        in_specs.append(pl.BlockSpec(memory_space=pl.ANY))
    return pl.pallas_call(
        functools.partial(factor_kernel, pieces=pieces, scale=scale),
        grid_spec=pltpu.PrefetchScalarGridSpec(
            num_scalar_prefetch=1,
            grid=(blocks,),
            in_specs=in_specs,
            out_specs=pl.BlockSpec((rank, step), lambda i, *_: (0, first + i)),
            scratch_shapes=[pltpu.VMEM((sum(t.shape[0] for t in tokens), rank), jnp.bfloat16)],
        ),
        out_shape=jax.ShapeDtypeStruct((rank, depth), jnp.float32),
        input_output_aliases=aliases,
        compiler_params=pltpu.CompilerParams(vmem_limit_bytes=vmem_bytes),
        cost_estimate=light,
        name="factor_gradient",
    )(order, *operands)


def scatter_send(state, hop):
    if hop == 0:
        kept, sent = state
        half = kept.shape[2] // 2
        got = [swap(sent[:, :, side * half : (side + 1) * half], "wide", 1) for side in range(2)]
        return kept, got
    bits = bits_of("wide")[:-1]
    stay, got = [], []
    for part, order in zip(state, (bits, bits[::-1])):
        bit = order[hop - 1]
        stay.append({p: part[p] for p in part if not p & bit})
        away = jnp.stack([part[p | bit].astype(jnp.bfloat16) for p in stay[-1]])
        got.append(swap(away, "wide", 2 * bit))
    return stay, got


def scatter_take(flight, hop):
    stay, got = flight
    if hop == 0:
        half = stay.shape[2] // 2
        return [
            {p: stay[p, :, side * half : (side + 1) * half] + got[side][p] for p in range(stay.shape[0])}
            for side in range(2)
        ]
    return [{p: part[p] + new[i] for i, p in enumerate(part)} for part, new in zip(stay, got)]


def hold(*groups):
    leaves, tree = jax.tree.flatten(groups)
    return jax.tree.unflatten(tree, lax.optimization_barrier(leaves))


def cut_rows(owner_rows):
    sizes = [piece_rows] * (owner_rows // piece_rows)
    if not sizes:
        sizes = [owner_rows]
    sizes[0] += owner_rows - sum(sizes)
    starts = [sum(sizes[:i]) for i in range(len(sizes))]
    return list(zip(starts, sizes))


def shards(inputs, grad_out, w_base, adapter_down_matrix, b_factor):
    owner_rows = inputs.shape[0]
    owners = lax.axis_size("wide")
    groups = lax.axis_size("narrow")
    me_wide = lax.axis_index("wide")
    me_narrow = lax.axis_index("narrow")
    adapter_matrix = adapter_scale / (owner_rows * owners)
    share = grad_out.shape[0] // owner_rows
    rank = b_factor.shape[0]
    depth = grad_out.shape[1]
    wide_bits, narrow_bits = bits_of("wide"), bits_of("narrow")
    pieces = cut_rows(owner_rows)
    count = len(pieces)
    line = groups == 4

    held = [me_narrow ^ i if line else jnp.int32(i) for i in range(groups)]
    table = [(block * share + h) ^ me_wide for block in held for h in range(share)]
    order = jnp.stack([block * share + h for block in held for h in range(share)]).astype(jnp.int32)
    table.append(((me_narrow == 0) | (me_narrow == groups - 1)).astype(jnp.int32))
    table = jnp.stack([entry.astype(jnp.int32) for entry in table])

    def block_of(source, i):
        start, rows = pieces[i]
        own = source.reshape(share, owner_rows, depth)
        return own[:, start : start + rows].reshape(share * rows, depth)

    blocks, near, far, middle, onward = {}, {}, {}, {}, {}

    def begin(i):
        if line:
            near[i], far[i] = phase_a(blocks[i], "narrow")
        else:
            near[i] = far[i] = lax.all_gather(blocks[i], "narrow", axis=0, tiled=True)

    def complete(i):
        if line:
            middle[i], onward[i] = phase_b(blocks[i], far[i], "narrow")
        else:
            middle[i], onward[i] = near[i], far[i]

    blocks[0] = block_of(grad_out, 0)
    begin(0)

    blocks[0], low_source = hold(blocks[0], grad_out)
    low_part = contract_trailing_axis(low_source, b_factor)
    low_small = scatter_small(low_part, "wide").astype(jnp.bfloat16)

    low_rows = low_small
    near[0], far[0], blocks[0], grad_out, low_rows, inputs = hold(
        near[0], far[0], blocks[0], grad_out, low_rows, inputs
    )
    complete(0)
    blocks[1] = block_of(grad_out, 1)
    act_part = jnp.dot(inputs, adapter_down_matrix, preferred_element_type=jnp.float32)
    both = jnp.concatenate([act_part.astype(jnp.bfloat16), low_rows], axis=0)
    small = {"inputs": inputs, "both": both}
    small["got"] = [swap(both, "narrow", p) for p in range(1, groups)]

    def take():
        if "both" in small:
            value = jnp.stack([small.pop("both"), *small.pop("got")])
            for bit in narrow_bits:
                cut = value.reshape(groups // (2 * bit), 2, bit, *value.shape[1:])
                value = jnp.where((me_narrow & bit) != 0, cut[:, ::-1], cut).reshape(value.shape)
            act = jnp.sum(value[:, :owner_rows].astype(jnp.float32), axis=0).astype(jnp.bfloat16)
            low = value[:, owner_rows:].reshape(-1, rank)
            small["rows"] = jnp.concatenate([act, low], axis=0)[None]
        elif "got" in small:
            upper = (me_wide & taken.pop(0)) != 0
            name = "rows" if "rows" in small else "grad_a"
            mine, other = small[name], small.pop("got")
            first, second = jnp.where(upper, other, mine), jnp.where(upper, mine, other)
            small[name] = jnp.concatenate([first, second], axis=0)

    taken = wide_bits + wide_bits[::-1]
    bits_left = list(taken)

    def small_hop():
        take()
        if not bits_left:
            return
        prepare()
        if "low_all" in small:
            share_made()
        small["got"] = swap(small["rows" if "rows" in small else "grad_a"], "wide", bits_left.pop(0))

    def prepare():
        if len(bits_left) <= len(wide_bits) and "rows" in small:
            take()
            rows_made()

    def regroup():
        shares = small.pop("inputs").reshape(owner_rows, owners, -1)
        flipped = [
            sum(bit for i, bit in enumerate(wide_bits) if w & wide_bits[len(wide_bits) - 1 - i])
            for w in range(owners)
        ]
        shares = jnp.stack([shares[:, f] for f in flipped], axis=0)
        columns = lax.all_to_all(shares, "wide", split_axis=0, concat_axis=0)
        small["columns"] = columns.reshape(owner_rows * owners, -1)

    def rows_made():
        rows = small.pop("rows")
        low_wide = rows[:, owner_rows:].reshape(owners, groups, low_small.shape[0], rank)
        small["low_all"] = jnp.swapaxes(low_wide, 0, 1).reshape(owner_rows * owners, rank)
        small["acts"] = rows[:, :owner_rows]

    def share_made():
        low_all = small.pop("low_all")
        low_own = lax.dynamic_slice_in_dim(low_all, me_wide * owner_rows, owner_rows)
        small["term"] = adapter_scale * contract_trailing_axis(low_own, adapter_down_matrix)
        made = adapter_matrix * contract_first(small.pop("columns"), low_all)
        small["grad_a"] = made.astype(jnp.bfloat16)

    tokens, sums = {}, {}
    done_hops = {}

    def sum_hop(i):
        if done_hops[i]:
            sums[i] = scatter_take(sums[i], done_hops[i] - 1)
        if done_hops[i] < len(wide_bits):
            sums[i] = scatter_send(sums[i], done_hops[i])
        done_hops[i] += 1

    def step(small_hops=1):
        for _ in range(small_hops):
            small_hop()
        for i in sums:
            if done_hops[i] <= len(wide_bits):
                sum_hop(i)

    def run_pass(i):
        sources = [blocks[i], near[i], far[i], middle[i], onward[i]] if line else [near[i]]
        tokens[i], kept, sent = weight_pass(table, sources, w_base, owners)
        sums[i] = (kept, sent)
        done_hops[i] = 0
        if i + 2 == count:
            sum_hop(i)

    regroup()
    for i in range(count):
        if i:
            near[i], far[i], blocks, grad_out, small, sums = hold(
                near[i], far[i], blocks, grad_out, small, sums
            )
            complete(i)
            if i + 1 < count:
                blocks[i + 1] = block_of(grad_out, i + 1)
            step(2 if i == 1 else 1)
            if i == 1 and count > 2:
                sum_hop(0)
        middle[i], onward[i], blocks, grad_out, small, sums = hold(
            middle[i], onward[i], blocks, grad_out, small, sums
        )
        if i + 1 < count:
            begin(i + 1)
            step(1 if i == 0 else 0)
            prepare()
            run_pass(i)
    step()
    run_pass(count - 1)
    small, sums = hold(small, sums)
    columns_step = max(128 * c for c in range(1, 14) if depth % (128 * c) == 0)
    steps = depth // columns_step
    early = steps // 2 or 1
    tokens = [tokens[i] for i in range(count)]
    last = count - 1

    def factor(first, blocks, into=None):
        return factor_gradient(
            order, small["acts"], tokens, pieces, adapter_matrix, columns_step, first, blocks, into
        )

    sum_hop(last)
    while bits_left or "got" in small:
        small_hop()
    grad_a = small["grad_a"].astype(jnp.float32)
    grad_b = factor(0, early)
    sum_hop(last)
    sums[last], grad_a, grad_b = hold(sums[last], grad_a, grad_b)
    if steps > early:
        grad_b = factor(early, steps - early, grad_b)
    results = []
    for i, (start, rows) in enumerate(pieces):
        while done_hops[i] <= len(wide_bits):
            sum_hop(i)
        mine = small["term"][start : start + rows]
        summed = jnp.concatenate([part[0] for part in sums[i]], axis=1)
        results.append((summed + mine).astype(jnp.bfloat16))
    return (jnp.concatenate(results, axis=0), grad_a, grad_b)


def solution(mesh):
    return jax.shard_map(
        shards,
        mesh=mesh,
        in_specs=(
            P("wide", "narrow"),
            P("narrow", "wide"),
            P("narrow", "wide"),
            P("narrow", None),
            P(None, "wide"),
        ),
        out_specs=(P("wide", "narrow"), P("narrow", None), P(None, "wide")),
        check_vma=False,
    )
```

```python
import functools

import jax
import jax.numpy as jnp
from jax import lax
from jax.experimental import pallas as pl
from jax.experimental.pallas import tpu as pltpu
from jax.sharding import PartitionSpec as P

adapter_scale = 2.0
piece_rows = 32
weight_rows = 512
vmem_bytes = 40 * 2**20
light = pl.CostEstimate(flops=0, bytes_accessed=2**16, transcendentals=0)


def contract_trailing_axis(left, right):
    return lax.dot_general(
        left, right, (((1,), (1,)), ((), ())), preferred_element_type=jnp.float32
    )


def contract_first(left, right):
    return lax.dot_general(
        left, right, (((0,), (0,)), ((), ())), preferred_element_type=jnp.float32
    )


def bits_of(axis):
    size = lax.axis_size(axis)
    return [1 << i for i in range(size.bit_length() - 1)]


def swap(value, axis, bit):
    size = lax.axis_size(axis)
    return lax.ppermute(value, axis, [(i, i ^ bit) for i in range(size)])


def scatter_small(value, axis):
    me = lax.axis_index(axis)
    for bit in reversed(bits_of(axis)):
        pair = value.reshape(2, value.shape[0] // 2, value.shape[1])
        mine = ((me & bit) != 0).astype(jnp.int32)
        kept = lax.dynamic_index_in_dim(pair, mine, 0, keepdims=False)
        sent = lax.dynamic_index_in_dim(pair, 1 - mine, 0, keepdims=False)
        value = kept + swap(sent, axis, bit)
    return value


def gather_ordered(value, axis, order):
    me = lax.axis_index(axis)
    for bit in order:
        other = swap(value, axis, bit)
        upper = (me & bit) != 0
        value = jnp.concatenate(
            [jnp.where(upper, other, value), jnp.where(upper, value, other)], axis=0
        )
    return value


def phase_a(block, axis):
    return swap(block, axis, 1), swap(block, axis, 2)


def phase_b(block, far, axis):
    return (
        lax.ppermute(block, axis, [(1, 2), (2, 1)]),
        lax.ppermute(far, axis, [(1, 0), (2, 3)]),
    )


def pass_kernel(table, *refs, sources, owners, rows):
    source_refs, refs = refs[:sources], refs[sources:]
    weight, refs = refs[0], refs[1:]
    if sources > 1:
        tokens, kept, sent = refs

        @pl.when(pl.program_id(0) == 0)
        def _():
            size = source_refs[0].shape[0]
            for i, source in enumerate(source_refs[: sources - 2]):
                tokens[i * size : (i + 1) * size] = source[...]
            for end in range(2):

                @pl.when(table[owners] == end)
                def _():
                    tokens[(sources - 2) * size :] = source_refs[sources - 2 + end][...]
    else:
        (tokens,) = source_refs
        kept, sent = refs
    product = contract_trailing_axis(tokens[...], weight[...])
    for i in range(owners):
        place = table[i]
        part = product[i * rows : (i + 1) * rows]

        @pl.when((place & 1) == 0)
        def _():
            kept[place >> 1] = part

        @pl.when((place & 1) == 1)
        def _():
            sent[place >> 1] = part.astype(jnp.bfloat16)


def weight_pass(table, sources, weight, owners):
    depth = weight.shape[1]
    width = weight.shape[0]
    total = sources[0].shape[0] * max(1, len(sources) - 1)
    rows = total // owners
    step = min(weight_rows, width)
    whole = lambda i, *_: (0, 0)
    once = pl.Buffered(1)
    in_specs = [pl.BlockSpec(s.shape, whole, pipeline_mode=once) for s in sources]
    in_specs.append(pl.BlockSpec((step, depth), lambda i, *_: (i, 0)))
    half = (owners // 2, rows, width)
    out_shape = [
        jax.ShapeDtypeStruct(half, jnp.float32),
        jax.ShapeDtypeStruct(half, jnp.bfloat16),
    ]
    out_specs = [pl.BlockSpec((owners // 2, rows, step), lambda i, *_: (0, 0, i))] * 2
    if len(sources) > 1:
        out_shape.insert(0, jax.ShapeDtypeStruct((total, depth), jnp.bfloat16))
        out_specs.insert(0, pl.BlockSpec((total, depth), whole, pipeline_mode=once))
    outs = pl.pallas_call(
        functools.partial(pass_kernel, sources=len(sources), owners=owners, rows=rows),
        grid_spec=pltpu.PrefetchScalarGridSpec(
            num_scalar_prefetch=1,
            grid=(width // step,),
            in_specs=in_specs,
            out_specs=out_specs,
        ),
        out_shape=out_shape,
        compiler_params=pltpu.CompilerParams(vmem_limit_bytes=vmem_bytes),
        cost_estimate=light,
        name="weight_pass",
    )(table, *sources, weight)
    return outs if len(sources) > 1 else [sources[0], *outs]


def factor_kernel(order, acts, *refs, pieces, scale):
    tokens, out, lined = refs[: len(pieces)], refs[-2], refs[-1]
    owners = acts.shape[0]

    @pl.when(pl.program_id(0) == 0)
    def _():
        base = 0
        for start, rows in pieces:
            for i in range(owners):
                lined[base : base + rows] = acts[order[i], start : start + rows, :]
                base += rows

    base, total = 0, None
    for token in tokens:
        size = token.shape[0]
        part = contract_first(lined[base : base + size], token[...])
        total = part if total is None else total + part
        base += size
    out[...] = scale * total


def factor_gradient(order, acts, tokens, pieces, scale, step, first, blocks, into=None):
    rank, depth = acts.shape[2], tokens[0].shape[1]
    in_specs = [
        pl.BlockSpec(acts.shape, lambda i, *_: (0, 0, 0), pipeline_mode=pl.Buffered(1))
    ]
    in_specs += [pl.BlockSpec((t.shape[0], step), lambda i, *_: (0, first + i)) for t in tokens]
    operands = [acts, *tokens]
    aliases = {}
    if into is not None:
        aliases = {1 + len(operands): 0}
        operands.append(into)
        in_specs.append(pl.BlockSpec(memory_space=pl.ANY))
    return pl.pallas_call(
        functools.partial(factor_kernel, pieces=pieces, scale=scale),
        grid_spec=pltpu.PrefetchScalarGridSpec(
            num_scalar_prefetch=1,
            grid=(blocks,),
            in_specs=in_specs,
            out_specs=pl.BlockSpec((rank, step), lambda i, *_: (0, first + i)),
            scratch_shapes=[pltpu.VMEM((sum(t.shape[0] for t in tokens), rank), jnp.bfloat16)],
        ),
        out_shape=jax.ShapeDtypeStruct((rank, depth), jnp.float32),
        input_output_aliases=aliases,
        compiler_params=pltpu.CompilerParams(vmem_limit_bytes=vmem_bytes),
        cost_estimate=light,
        name="factor_gradient",
    )(order, *operands)


def scatter_send(state, hop):
    if hop == 0:
        kept, sent = state
        half = kept.shape[2] // 2
        got = [swap(sent[:, :, side * half : (side + 1) * half], "wide", 1) for side in range(2)]
        return kept, got
    bits = bits_of("wide")[:-1]
    stay, got = [], []
    for part, order in zip(state, (bits, bits[::-1])):
        bit = order[hop - 1]
        stay.append({p: part[p] for p in part if not p & bit})
        away = jnp.stack([part[p | bit].astype(jnp.bfloat16) for p in stay[-1]])
        got.append(swap(away, "wide", 2 * bit))
    return stay, got


def scatter_take(flight, hop):
    stay, got = flight
    if hop == 0:
        half = stay.shape[2] // 2
        return [
            {p: stay[p, :, side * half : (side + 1) * half] + got[side][p] for p in range(stay.shape[0])}
            for side in range(2)
        ]
    return [{p: part[p] + new[i] for i, p in enumerate(part)} for part, new in zip(stay, got)]


def hold(*groups):
    leaves, tree = jax.tree.flatten(groups)
    return jax.tree.unflatten(tree, lax.optimization_barrier(leaves))


def cut_rows(owner_rows):
    sizes = [piece_rows] * (owner_rows // piece_rows)
    if not sizes:
        sizes = [owner_rows]
    sizes[0] += owner_rows - sum(sizes)
    starts = [sum(sizes[:i]) for i in range(len(sizes))]
    return list(zip(starts, sizes))


def shards(inputs, grad_out, w_base, adapter_down_matrix, b_factor):
    owner_rows = inputs.shape[0]
    owners = lax.axis_size("wide")
    groups = lax.axis_size("narrow")
    me_wide = lax.axis_index("wide")
    me_narrow = lax.axis_index("narrow")
    adapter_matrix = adapter_scale / (owner_rows * owners)
    share = grad_out.shape[0] // owner_rows
    rank = b_factor.shape[0]
    depth = grad_out.shape[1]
    wide_bits, narrow_bits = bits_of("wide"), bits_of("narrow")
    pieces = cut_rows(owner_rows)
    count = len(pieces)
    line = groups == 4

    held = [me_narrow ^ i if line else jnp.int32(i) for i in range(groups)]
    table = [(block * share + h) ^ me_wide for block in held for h in range(share)]
    order = jnp.stack([block * share + h for block in held for h in range(share)]).astype(jnp.int32)
    table.append(((me_narrow == 0) | (me_narrow == groups - 1)).astype(jnp.int32))
    table = jnp.stack([entry.astype(jnp.int32) for entry in table])

    def block_of(source, i):
        start, rows = pieces[i]
        own = source.reshape(share, owner_rows, depth)
        return own[:, start : start + rows].reshape(share * rows, depth)

    blocks, near, far, middle, onward = {}, {}, {}, {}, {}

    def begin(i):
        if line:
            near[i], far[i] = phase_a(blocks[i], "narrow")
        else:
            near[i] = far[i] = lax.all_gather(blocks[i], "narrow", axis=0, tiled=True)

    def complete(i):
        if line:
            middle[i], onward[i] = phase_b(blocks[i], far[i], "narrow")
        else:
            middle[i], onward[i] = near[i], far[i]

    blocks[0] = block_of(grad_out, 0)
    begin(0)

    blocks[0], low_source = hold(blocks[0], grad_out)
    low_part = contract_trailing_axis(low_source, b_factor)
    low_small = scatter_small(low_part, "wide").astype(jnp.bfloat16)

    low_rows = low_small
    near[0], far[0], blocks[0], grad_out, low_rows, inputs = hold(
        near[0], far[0], blocks[0], grad_out, low_rows, inputs
    )
    complete(0)
    blocks[1] = block_of(grad_out, 1)
    act_part = jnp.dot(inputs, adapter_down_matrix, preferred_element_type=jnp.float32)
    both = jnp.concatenate([act_part.astype(jnp.bfloat16), low_rows], axis=0)
    small = {"inputs": inputs, "both": both}
    small["got"] = [swap(both, "narrow", p) for p in range(1, groups)]

    def take():
        if "both" in small:
            value = jnp.stack([small.pop("both"), *small.pop("got")])
            for bit in narrow_bits:
                cut = value.reshape(groups // (2 * bit), 2, bit, *value.shape[1:])
                value = jnp.where((me_narrow & bit) != 0, cut[:, ::-1], cut).reshape(value.shape)
            act = jnp.sum(value[:, :owner_rows].astype(jnp.float32), axis=0).astype(jnp.bfloat16)
            low = value[:, owner_rows:].reshape(-1, rank)
            small["rows"] = jnp.concatenate([act, low], axis=0)[None]
        elif "got" in small:
            upper = (me_wide & taken.pop(0)) != 0
            name = "rows" if "rows" in small else "grad_a"
            mine, other = small[name], small.pop("got")
            first, second = jnp.where(upper, other, mine), jnp.where(upper, mine, other)
            small[name] = jnp.concatenate([first, second], axis=0)

    taken = wide_bits + wide_bits[::-1]
    bits_left = list(taken)

    def small_hop():
        take()
        if not bits_left:
            return
        prepare()
        if "low_all" in small:
            share_made()
        small["got"] = swap(small["rows" if "rows" in small else "grad_a"], "wide", bits_left.pop(0))

    def prepare():
        if len(bits_left) <= len(wide_bits) and "rows" in small:
            take()
            rows_made()

    def regroup():
        shares = small.pop("inputs").reshape(owner_rows, owners, -1)
        flipped = [
            sum(bit for i, bit in enumerate(wide_bits) if w & wide_bits[len(wide_bits) - 1 - i])
            for w in range(owners)
        ]
        shares = jnp.stack([shares[:, f] for f in flipped], axis=0)
        columns = lax.all_to_all(shares, "wide", split_axis=0, concat_axis=0)
        small["columns"] = columns.reshape(owner_rows * owners, -1)

    def rows_made():
        rows = small.pop("rows")
        low_wide = rows[:, owner_rows:].reshape(owners, groups, low_small.shape[0], rank)
        small["low_all"] = jnp.swapaxes(low_wide, 0, 1).reshape(owner_rows * owners, rank)
        small["acts"] = rows[:, :owner_rows]

    def share_made():
        low_all = small.pop("low_all")
        low_own = lax.dynamic_slice_in_dim(low_all, me_wide * owner_rows, owner_rows)
        small["term"] = adapter_scale * contract_trailing_axis(low_own, adapter_down_matrix)
        made = adapter_matrix * contract_first(small.pop("columns"), low_all)
        small["grad_a"] = made.astype(jnp.bfloat16)

    tokens, sums = {}, {}
    done_hops = {}

    def sum_hop(i):
        if done_hops[i]:
            sums[i] = scatter_take(sums[i], done_hops[i] - 1)
        if done_hops[i] < len(wide_bits):
            sums[i] = scatter_send(sums[i], done_hops[i])
        done_hops[i] += 1

    def step(small_hops=1):
        for _ in range(small_hops):
            small_hop()
        for i in sums:
            if done_hops[i] <= len(wide_bits):
                sum_hop(i)

    def run_pass(i):
        sources = [blocks[i], near[i], far[i], middle[i], onward[i]] if line else [near[i]]
        tokens[i], kept, sent = weight_pass(table, sources, w_base, owners)
        sums[i] = (kept, sent)
        done_hops[i] = 0
        if i + 2 == count:
            sum_hop(i)

    regroup()
    for i in range(count):
        if i:
            near[i], far[i], blocks, grad_out, small, sums = hold(
                near[i], far[i], blocks, grad_out, small, sums
            )
            complete(i)
            if i + 1 < count:
                blocks[i + 1] = block_of(grad_out, i + 1)
            step(2 if i == 1 else 1)
            if i == 1 and count > 2:
                sum_hop(0)
            if i + 1 == count:
                step()
        middle[i], onward[i], blocks, grad_out, small, sums = hold(
            middle[i], onward[i], blocks, grad_out, small, sums
        )
        if i + 1 < count:
            begin(i + 1)
            step(1 if i == 0 else 0)
            prepare()
            run_pass(i)
    run_pass(count - 1)
    small, sums = hold(small, sums)
    columns_step = max(128 * c for c in range(1, 14) if depth % (128 * c) == 0)
    steps = depth // columns_step
    early = steps // 2 or 1
    tokens = [tokens[i] for i in range(count)]
    last = count - 1

    def factor(first, blocks, into=None):
        return factor_gradient(
            order, small["acts"], tokens, pieces, adapter_matrix, columns_step, first, blocks, into
        )

    sum_hop(last)
    while bits_left or "got" in small:
        small_hop()
    grad_a = small["grad_a"].astype(jnp.float32)
    grad_b = factor(0, early)
    sum_hop(last)
    sums[last], grad_a, grad_b = hold(sums[last], grad_a, grad_b)
    if steps > early:
        grad_b = factor(early, steps - early, grad_b)
    results = []
    for i, (start, rows) in enumerate(pieces):
        while done_hops[i] <= len(wide_bits):
            sum_hop(i)
        mine = small["term"][start : start + rows]
        summed = jnp.concatenate([part[0] for part in sums[i]], axis=1)
        results.append((summed + mine).astype(jnp.bfloat16))
    return (jnp.concatenate(results, axis=0), grad_a, grad_b)


def solution(mesh):
    return jax.shard_map(
        shards,
        mesh=mesh,
        in_specs=(
            P("wide", "narrow"),
            P("narrow", "wide"),
            P("narrow", "wide"),
            P("narrow", None),
            P(None, "wide"),
        ),
        out_specs=(P("wide", "narrow"), P("narrow", None), P(None, "wide")),
        check_vma=False,
    )
```

```python
import functools

import jax
import jax.numpy as jnp
from jax import lax
from jax.experimental import pallas as pl
from jax.experimental.pallas import tpu as pltpu
from jax.sharding import PartitionSpec as P

adapter_scale = 2.0
piece_rows = 32
weight_rows = 512
vmem_bytes = 40 * 2**20
light = pl.CostEstimate(flops=0, bytes_accessed=2**16, transcendentals=0)


def contract_trailing_axis(left, right):
    return lax.dot_general(
        left, right, (((1,), (1,)), ((), ())), preferred_element_type=jnp.float32
    )


def contract_first(left, right):
    return lax.dot_general(
        left, right, (((0,), (0,)), ((), ())), preferred_element_type=jnp.float32
    )


def bits_of(axis):
    size = lax.axis_size(axis)
    return [1 << i for i in range(size.bit_length() - 1)]


def swap(value, axis, bit):
    size = lax.axis_size(axis)
    return lax.ppermute(value, axis, [(i, i ^ bit) for i in range(size)])


def scatter_small(value, axis):
    me = lax.axis_index(axis)
    for bit in reversed(bits_of(axis)):
        pair = value.reshape(2, value.shape[0] // 2, value.shape[1])
        mine = ((me & bit) != 0).astype(jnp.int32)
        kept = lax.dynamic_index_in_dim(pair, mine, 0, keepdims=False)
        sent = lax.dynamic_index_in_dim(pair, 1 - mine, 0, keepdims=False)
        value = kept + swap(sent, axis, bit)
    return value


def gather_ordered(value, axis, order):
    me = lax.axis_index(axis)
    for bit in order:
        other = swap(value, axis, bit)
        upper = (me & bit) != 0
        value = jnp.concatenate(
            [jnp.where(upper, other, value), jnp.where(upper, value, other)], axis=0
        )
    return value


def phase_a(block, axis):
    return swap(block, axis, 1), swap(block, axis, 2)


def phase_b(block, far, axis):
    return (
        lax.ppermute(block, axis, [(1, 2), (2, 1)]),
        lax.ppermute(far, axis, [(1, 0), (2, 3)]),
    )


def pass_kernel(table, *refs, sources, owners, rows):
    source_refs, refs = refs[:sources], refs[sources:]
    weight, refs = refs[0], refs[1:]
    if sources > 1:
        tokens, kept, sent = refs

        @pl.when(pl.program_id(0) == 0)
        def _():
            size = source_refs[0].shape[0]
            for i, source in enumerate(source_refs[: sources - 2]):
                tokens[i * size : (i + 1) * size] = source[...]
            for end in range(2):

                @pl.when(table[owners] == end)
                def _():
                    tokens[(sources - 2) * size :] = source_refs[sources - 2 + end][...]
    else:
        (tokens,) = source_refs
        kept, sent = refs
    product = contract_trailing_axis(tokens[...], weight[...])
    for i in range(owners):
        place = table[i]
        part = product[i * rows : (i + 1) * rows]

        @pl.when((place & 1) == 0)
        def _():
            kept[place >> 1] = part

        @pl.when((place & 1) == 1)
        def _():
            sent[place >> 1] = part.astype(jnp.bfloat16)


def weight_pass(table, sources, weight, owners):
    depth = weight.shape[1]
    width = weight.shape[0]
    total = sources[0].shape[0] * max(1, len(sources) - 1)
    rows = total // owners
    step = min(weight_rows, width)
    whole = lambda i, *_: (0, 0)
    once = pl.Buffered(1)
    in_specs = [pl.BlockSpec(s.shape, whole, pipeline_mode=once) for s in sources]
    in_specs.append(pl.BlockSpec((step, depth), lambda i, *_: (i, 0)))
    half = (owners // 2, rows, width)
    out_shape = [
        jax.ShapeDtypeStruct(half, jnp.float32),
        jax.ShapeDtypeStruct(half, jnp.bfloat16),
    ]
    out_specs = [pl.BlockSpec((owners // 2, rows, step), lambda i, *_: (0, 0, i))] * 2
    if len(sources) > 1:
        out_shape.insert(0, jax.ShapeDtypeStruct((total, depth), jnp.bfloat16))
        out_specs.insert(0, pl.BlockSpec((total, depth), whole, pipeline_mode=once))
    outs = pl.pallas_call(
        functools.partial(pass_kernel, sources=len(sources), owners=owners, rows=rows),
        grid_spec=pltpu.PrefetchScalarGridSpec(
            num_scalar_prefetch=1,
            grid=(width // step,),
            in_specs=in_specs,
            out_specs=out_specs,
        ),
        out_shape=out_shape,
        compiler_params=pltpu.CompilerParams(vmem_limit_bytes=vmem_bytes),
        cost_estimate=light,
        name="weight_pass",
    )(table, *sources, weight)
    return outs if len(sources) > 1 else [sources[0], *outs]


def factor_kernel(order, acts, *refs, pieces, scale):
    tokens, out, lined = refs[: len(pieces)], refs[-2], refs[-1]
    owners = acts.shape[0]

    @pl.when(pl.program_id(0) == 0)
    def _():
        base = 0
        for start, rows in pieces:
            for i in range(owners):
                lined[base : base + rows] = acts[order[i], start : start + rows, :]
                base += rows

    base, total = 0, None
    for token in tokens:
        size = token.shape[0]
        part = contract_first(lined[base : base + size], token[...])
        total = part if total is None else total + part
        base += size
    out[...] = scale * total


def factor_gradient(order, acts, tokens, pieces, scale, step, first, blocks, into=None):
    rank, depth = acts.shape[2], tokens[0].shape[1]
    in_specs = [
        pl.BlockSpec(acts.shape, lambda i, *_: (0, 0, 0), pipeline_mode=pl.Buffered(1))
    ]
    in_specs += [pl.BlockSpec((t.shape[0], step), lambda i, *_: (0, first + i)) for t in tokens]
    operands = [acts, *tokens]
    aliases = {}
    if into is not None:
        aliases = {1 + len(operands): 0}
        operands.append(into)
        in_specs.append(pl.BlockSpec(memory_space=pl.ANY))
    return pl.pallas_call(
        functools.partial(factor_kernel, pieces=pieces, scale=scale),
        grid_spec=pltpu.PrefetchScalarGridSpec(
            num_scalar_prefetch=1,
            grid=(blocks,),
            in_specs=in_specs,
            out_specs=pl.BlockSpec((rank, step), lambda i, *_: (0, first + i)),
            scratch_shapes=[pltpu.VMEM((sum(t.shape[0] for t in tokens), rank), jnp.bfloat16)],
        ),
        out_shape=jax.ShapeDtypeStruct((rank, depth), jnp.float32),
        input_output_aliases=aliases,
        compiler_params=pltpu.CompilerParams(vmem_limit_bytes=vmem_bytes),
        cost_estimate=light,
        name="factor_gradient",
    )(order, *operands)


def scatter_send(state, hop):
    if hop == 0:
        kept, sent = state
        half = kept.shape[2] // 2
        got = [swap(sent[:, :, side * half : (side + 1) * half], "wide", 1) for side in range(2)]
        return kept, got
    bits = bits_of("wide")[:-1]
    stay, got = [], []
    for part, order in zip(state, (bits, bits[::-1])):
        bit = order[hop - 1]
        stay.append({p: part[p] for p in part if not p & bit})
        away = jnp.stack([part[p | bit].astype(jnp.bfloat16) for p in stay[-1]])
        got.append(swap(away, "wide", 2 * bit))
    return stay, got


def scatter_take(flight, hop):
    stay, got = flight
    if hop == 0:
        half = stay.shape[2] // 2
        return [
            {p: stay[p, :, side * half : (side + 1) * half] + got[side][p] for p in range(stay.shape[0])}
            for side in range(2)
        ]
    return [{p: part[p] + new[i] for i, p in enumerate(part)} for part, new in zip(stay, got)]


def hold(*groups):
    leaves, tree = jax.tree.flatten(groups)
    return jax.tree.unflatten(tree, lax.optimization_barrier(leaves))


def cut_rows(owner_rows):
    sizes = [piece_rows] * (owner_rows // piece_rows)
    if not sizes:
        sizes = [owner_rows]
    sizes[0] += owner_rows - sum(sizes)
    starts = [sum(sizes[:i]) for i in range(len(sizes))]
    return list(zip(starts, sizes))


def shards(inputs, grad_out, w_base, adapter_down_matrix, b_factor):
    owner_rows = inputs.shape[0]
    owners = lax.axis_size("wide")
    groups = lax.axis_size("narrow")
    me_wide = lax.axis_index("wide")
    me_narrow = lax.axis_index("narrow")
    adapter_matrix = adapter_scale / (owner_rows * owners)
    share = grad_out.shape[0] // owner_rows
    rank = b_factor.shape[0]
    depth = grad_out.shape[1]
    wide_bits, narrow_bits = bits_of("wide"), bits_of("narrow")
    pieces = cut_rows(owner_rows)
    count = len(pieces)
    line = groups == 4

    held = [me_narrow ^ i if line else jnp.int32(i) for i in range(groups)]
    table = [(block * share + h) ^ me_wide for block in held for h in range(share)]
    order = jnp.stack([block * share + h for block in held for h in range(share)]).astype(jnp.int32)
    table.append(((me_narrow == 0) | (me_narrow == groups - 1)).astype(jnp.int32))
    table = jnp.stack([entry.astype(jnp.int32) for entry in table])

    def block_of(source, i):
        start, rows = pieces[i]
        own = source.reshape(share, owner_rows, depth)
        return own[:, start : start + rows].reshape(share * rows, depth)

    blocks, near, far, middle, onward = {}, {}, {}, {}, {}

    def begin(i):
        if line:
            near[i], far[i] = phase_a(blocks[i], "narrow")
        else:
            near[i] = far[i] = lax.all_gather(blocks[i], "narrow", axis=0, tiled=True)

    def complete(i):
        if line:
            middle[i], onward[i] = phase_b(blocks[i], far[i], "narrow")
        else:
            middle[i], onward[i] = near[i], far[i]

    blocks[0] = block_of(grad_out, 0)
    begin(0)

    blocks[0], low_source = hold(blocks[0], grad_out)
    low_part = contract_trailing_axis(low_source, b_factor)
    low_small = scatter_small(low_part, "wide").astype(jnp.bfloat16)

    low_rows = low_small
    near[0], far[0], blocks[0], grad_out, low_rows, inputs = hold(
        near[0], far[0], blocks[0], grad_out, low_rows, inputs
    )
    complete(0)
    blocks[1] = block_of(grad_out, 1)
    act_part = jnp.dot(inputs, adapter_down_matrix, preferred_element_type=jnp.float32)
    both = jnp.concatenate([act_part.astype(jnp.bfloat16), low_rows], axis=0)
    small = {"inputs": inputs, "both": both}
    small["got"] = [swap(both, "narrow", p) for p in range(1, groups)]

    def take():
        if "both" in small:
            value = jnp.stack([small.pop("both"), *small.pop("got")])
            for bit in narrow_bits:
                cut = value.reshape(groups // (2 * bit), 2, bit, *value.shape[1:])
                value = jnp.where((me_narrow & bit) != 0, cut[:, ::-1], cut).reshape(value.shape)
            act = jnp.sum(value[:, :owner_rows].astype(jnp.float32), axis=0).astype(jnp.bfloat16)
            low = value[:, owner_rows:].reshape(-1, rank)
            small["rows"] = jnp.concatenate([act, low], axis=0)[None]
        elif "got" in small:
            upper = (me_wide & taken.pop(0)) != 0
            name = "rows" if "rows" in small else "grad_a"
            mine, other = small[name], small.pop("got")
            first, second = jnp.where(upper, other, mine), jnp.where(upper, mine, other)
            small[name] = jnp.concatenate([first, second], axis=0)

    taken = wide_bits + wide_bits[::-1]
    bits_left = list(taken)

    def small_hop():
        take()
        if not bits_left:
            return
        if len(bits_left) == len(wide_bits):
            share_made()
        small["got"] = swap(small["rows" if "rows" in small else "grad_a"], "wide", bits_left.pop(0))

    def regroup():
        shares = small.pop("inputs").reshape(owner_rows, owners, -1)
        flipped = [
            sum(bit for i, bit in enumerate(wide_bits) if w & wide_bits[len(wide_bits) - 1 - i])
            for w in range(owners)
        ]
        shares = jnp.stack([shares[:, f] for f in flipped], axis=0)
        columns = lax.all_to_all(shares, "wide", split_axis=0, concat_axis=0)
        small["columns"] = columns.reshape(owner_rows * owners, -1)

    def share_made():
        rows = small.pop("rows")
        low_wide = rows[:, owner_rows:].reshape(owners, groups, low_small.shape[0], rank)
        low_all = jnp.swapaxes(low_wide, 0, 1).reshape(owner_rows * owners, rank)
        low_own = lax.dynamic_slice_in_dim(low_all, me_wide * owner_rows, owner_rows)
        small["term"] = adapter_scale * contract_trailing_axis(low_own, adapter_down_matrix)
        made = adapter_matrix * contract_first(small.pop("columns"), low_all)
        small["grad_a"] = made.astype(jnp.bfloat16)
        small["acts"] = rows[:, :owner_rows]

    tokens, sums = {}, {}
    done_hops = {}

    def sum_hop(i):
        if done_hops[i]:
            sums[i] = scatter_take(sums[i], done_hops[i] - 1)
        if done_hops[i] < len(wide_bits):
            sums[i] = scatter_send(sums[i], done_hops[i])
        done_hops[i] += 1

    def step(small_hops=1):
        for _ in range(small_hops):
            small_hop()
        for i in sums:
            if done_hops[i] <= len(wide_bits):
                sum_hop(i)

    def run_pass(i):
        sources = [blocks[i], near[i], far[i], middle[i], onward[i]] if line else [near[i]]
        tokens[i], kept, sent = weight_pass(table, sources, w_base, owners)
        sums[i] = (kept, sent)
        done_hops[i] = 0
        if i + 2 == count:
            sums.update(hold(sums)[0])
            sum_hop(i)

    regroup()
    for i in range(count):
        if i:
            near[i], far[i], blocks, grad_out, small, sums = hold(
                near[i], far[i], blocks, grad_out, small, sums
            )
            complete(i)
            if i + 1 < count:
                blocks[i + 1] = block_of(grad_out, i + 1)
            step(2 if i == 1 else 1)
        middle[i], onward[i], blocks, grad_out, small, sums = hold(
            middle[i], onward[i], blocks, grad_out, small, sums
        )
        if i + 1 < count:
            begin(i + 1)
            step(1 if i == 0 else 0)
            run_pass(i)
    step()
    run_pass(count - 1)
    small, sums = hold(small, sums)
    columns_step = max(128 * c for c in range(1, 14) if depth % (128 * c) == 0)
    steps = depth // columns_step
    early = steps // 4 or 1
    tokens = [tokens[i] for i in range(count)]
    last = count - 1

    def factor(first, blocks, into=None):
        return factor_gradient(
            order, small["acts"], tokens, pieces, adapter_matrix, columns_step, first, blocks, into
        )

    sum_hop(last)
    while bits_left or "got" in small:
        small_hop()
    grad_a = small["grad_a"].astype(jnp.float32)
    grad_b = factor(0, early)
    sums[last], grad_b = hold(sums[last], grad_b)
    sum_hop(last)
    half = min(steps // 2, steps - early)
    if half:
        grad_b = factor(early, half, grad_b)
    sums[last], grad_a, grad_b = hold(sums[last], grad_a, grad_b)
    if steps > early + half:
        grad_b = factor(early + half, steps - early - half, grad_b)
    results = []
    for i, (start, rows) in enumerate(pieces):
        while done_hops[i] <= len(wide_bits):
            sum_hop(i)
        mine = small["term"][start : start + rows]
        summed = jnp.concatenate([part[0] for part in sums[i]], axis=1)
        results.append((summed + mine).astype(jnp.bfloat16))
    return (jnp.concatenate(results, axis=0), grad_a, grad_b)


def solution(mesh):
    return jax.shard_map(
        shards,
        mesh=mesh,
        in_specs=(
            P("wide", "narrow"),
            P("narrow", "wide"),
            P("narrow", "wide"),
            P("narrow", None),
            P(None, "wide"),
        ),
        out_specs=(P("wide", "narrow"), P("narrow", None), P(None, "wide")),
        check_vma=False,
    )
```
